768 devices in a mesh: node: 96 (over z, x, y_hi), local: 8 (over y_lo, core).
Axes of the slice: x: 4, y: 8 (y_hi: 2, y_lo: 4; y = y_hi * 4 + y_lo), z: 12, core: 2. Of those that a mesh axis runs over, the one named last changes fastest.
Arguments:
- hidden: bfloat16 [147456, 4608], P(('node', 'local')), may hold values from -24 to 24
- cotangent: bfloat16 [147456, 512], P(('node', 'local')), may hold values from -6 to 6
- quant_weight: bfloat16 [1152, 2048], P('node', 'local'), may hold values from -127 to 127
- scales: bfloat16 [1152], P('node'), may hold values from 9.9658966e-05 to 0.00039863586
Outputs:
- keys: bfloat16 [147456, 512], P(('node', 'local'))
- grad_input: bfloat16 [147456, 4608], P(('node', 'local'))
- weight_grad: float32 [1152, 2048], P('node', 'local')
The draws below stay inside these ranges and needn't reach their ends.
All inputs are finite; a program needn't handle non-finite values.
Results may differ from the reference program's by a relative error of at most 0.015.
Values may be sent and summed in bfloat16 or wider, within the bound.
No kernel may reach another device: no remote copies, remote signals or barrier semaphores. Data moves between devices by JAX's collectives and lax.ppermute only.
A program may use at most 64 MiB of HBM per device.

```python
import math
import jax
import jax.numpy as jnp
from jax import lax

D_IN = 4608
KVW = 512
BLK = 2048
TOK_DEV = 192
BLOCKS = 1152
TOKENS = 147456


def strengthened(drawn, stream_key, source, target, blocks, factor):
    owner, partner = [(jnp.arange(drawn.shape[axis_at]) // (drawn.shape[axis_at] // blocks)).reshape([-1 if axis == axis_at else 1 for axis in range(drawn.ndim)]) for axis_at in (source, target)]
    chosen = jax.random.permutation(stream_key, blocks)[partner]
    strong = (owner == chosen) | (owner == (partner + blocks // 2) % blocks)
    return jnp.where(strong, factor * drawn, drawn)


def level_of(key, dims, cuts, low, top_value):
    gain, own = 1.0, jax.random.fold_in(key, 6)
    for axis_at, blocks in cuts:
        steps = jnp.exp(jax.random.uniform(jax.random.fold_in(own, axis_at), (blocks,), jnp.float32, low / len(cuts), top_value / len(cuts)))
        gain = gain * jnp.repeat(steps, dims[axis_at] // blocks).reshape([-1 if axis == axis_at else 1 for axis in range(len(dims))])
    return gain


def centred(key, dims, scale, limit, pieces=(), held_as=jnp.bfloat16):
    entries = scale * jax.random.normal(key, dims, jnp.float32)
    if pieces:
        entries = entries * level_of(key, dims, pieces, -0.22, 0.18)
    return jnp.clip(entries, -limit, limit).astype(held_as)


def noise_with(rng, shape, spread, most, split, heavy, kind=jnp.bfloat16):
    array = spread * jax.random.normal(rng, shape, jnp.float32)
    if split:
        array = array * level_of(rng, shape, split, -0.22, 0.18)
    return jnp.clip(strengthened(array, jax.random.fold_in(rng, 3), *heavy), -most, most).astype(kind)


def setup_inputs(seed: int = 0) -> dict:
    streams_of = jax.random.split(jax.random.key(seed), 5)
    hidden = noise_with(streams_of[0], (TOKENS, D_IN), 1.0, 24.0, ((0, 768),), (0, 1, 768, 6.0))
    cotangent = centred(streams_of[1], (TOKENS, KVW), 1.0, 6.0, ((0, 768),))
    quant_weight = jnp.clip(jax.random.uniform(streams_of[2], (BLOCKS, BLK), jnp.float32, -127.0, 127.0) * level_of(streams_of[2], (BLOCKS, BLK), ((0, 96), (1, 8)), -0.4, 0.0), -127.0, 127.0).astype(jnp.bfloat16)
    scales = jnp.clip(jnp.exp(math.log(0.00039863586) - 1.3862944 * jax.random.uniform(streams_of[3], (BLOCKS,), jnp.float32) ** level_of(streams_of[3], (BLOCKS,), ((0, 96),), -0.2, 0.2)), 9.965896606445312e-05, 0.00039863586).astype(jnp.bfloat16)
    return dict(hidden=hidden, cotangent=cotangent, quant_weight=quant_weight, scales=scales)


def reference(hidden, cotangent, quant_weight, scales):
    weight = (quant_weight.astype(jnp.float32) * scales.astype(jnp.float32)[:, None]).astype(jnp.bfloat16)
    weight = weight.reshape(D_IN, KVW)
    keys = jnp.dot(hidden, weight, preferred_element_type=jnp.float32).astype(jnp.bfloat16)
    grad_input = lax.dot_general(cotangent, weight, (((1,), (1,)), ((), ())), preferred_element_type=jnp.float32).astype(jnp.bfloat16)
    groups = TOKENS // TOK_DEV
    hidden_groups = hidden.reshape(groups, TOK_DEV, D_IN)
    cot_groups = cotangent.reshape(groups, TOK_DEV, KVW)

    def accumulate(total, pair):
        term = lax.dot_general(pair[0], pair[1], (((0,), (0,)), ((), ())), preferred_element_type=jnp.float32)
        return (total + term.astype(jnp.bfloat16).astype(jnp.float32), None)
    total, unused = lax.scan(accumulate, jnp.zeros((D_IN, KVW), jnp.float32), (hidden_groups, cot_groups))
    weight_grad = (total * (1.0 / math.sqrt(TOKENS))).reshape(BLOCKS, BLK)
    return (keys, grad_input, weight_grad)
```

```python
import math

import jax
import jax.numpy as jnp
import numpy as np
from jax import lax
from jax.experimental import pallas as pl
from jax.experimental.pallas import tpu as pltpu
from jax.sharding import Mesh
from jax.sharding import PartitionSpec as P

NZ, NX, NYH, NYL, NC = 12, 4, 2, 4, 2
NY = NYH * NYL
Y = ("yh", "yl")
ROWS = 12
HALF = 256
ZROWS = NX * NY * ROWS
XROWS = NY * ROWS

BF = jnp.bfloat16
F32 = jnp.float32

_x, _yh, _i, _yl = np.meshgrid(
    np.arange(NX), np.arange(NYH), np.arange(ROWS), np.arange(NYL), indexing="ij"
)
_natural = (((_x * NYH + _yh) * ROWS + _i) * NYL + _yl).ravel()
_gathered = (((_yh * NYL + _yl) * NX + _x) * ROWS + _i).ravel()
_scattered = (((_x * NYH + _yh) * NYL + _yl) * ROWS + _i).ravel()
TO_NATURAL = np.zeros((ZROWS, ZROWS), np.float32)
TO_NATURAL[_natural, _gathered] = 1
TO_SCATTER = np.zeros((ZROWS, ZROWS), np.float32)
TO_SCATTER[_scattered, _natural] = 1
ZG = 4
_z, _y, _i2 = np.meshgrid(np.arange(ZG), np.arange(NY), np.arange(ROWS), indexing="ij")
TO_Y = np.zeros((ZROWS, ZROWS), np.float32)
TO_Y[((_y * ZG + _z) * ROWS + _i2).ravel(), ((_z * NY + _y) * ROWS + _i2).ravel()] = 1


def term_kernel(core, mine, other, cot_mine, cot_other, perm, out):
    dims = (((0,), (0,)), ((), ()))
    term = lax.dot_general(mine[...], cot_mine[...], dims, preferred_element_type=F32)
    term += lax.dot_general(other[...], cot_other[...], dims, preferred_element_type=F32)
    moved = jnp.dot(perm[...], term.astype(BF), preferred_element_type=F32)
    out[...] = moved.astype(BF).reshape(out.shape)


def chip_term(core, mine, other, cot_mine, cot_other):
    tokens, width = mine.shape
    return pl.pallas_call(
        term_kernel,
        grid_spec=pltpu.PrefetchScalarGridSpec(
            num_scalar_prefetch=1,
            grid=(NZ,),
            in_specs=[
                pl.BlockSpec((tokens, ZROWS), lambda z, core: (0, z)),
                pl.BlockSpec((tokens, ZROWS), lambda z, core: (0, z)),
                pl.BlockSpec((tokens, HALF), lambda z, core: (0, core[0])),
                pl.BlockSpec((tokens, HALF), lambda z, core: (0, core[0])),
                pl.BlockSpec((ZROWS, ZROWS), lambda z, core: (0, 0)),
            ],
            out_specs=pl.BlockSpec((NX, 1, XROWS, HALF), lambda z, core: (0, z, 0, 0)),
        ),
        out_shape=jax.ShapeDtypeStruct((NX, NZ, XROWS, HALF), BF),
        cost_estimate=pl.CostEstimate(
            flops=2 * width * HALF * (2 * tokens + ZROWS),
            bytes_accessed=4 * tokens * width + 2 * width * HALF,
            transcendentals=0,
        ),
        name="chip_term",
    )(core, mine, other, cot_mine, cot_other, jnp.asarray(TO_SCATTER, BF))


def sum_kernel(parts, perm, out):
    total = parts[0].astype(F32)
    for k in range(1, NX):
        total += parts[k].astype(F32)
    rows = total.astype(BF).reshape(ZROWS, HALF)
    moved = jnp.dot(perm[...], rows, preferred_element_type=F32)
    out[...] = moved.astype(BF).reshape(out.shape)


def sum_over_x(parts):
    return pl.pallas_call(
        sum_kernel,
        grid=(NZ // ZG,),
        in_specs=[
            pl.BlockSpec((NX, ZG, XROWS, HALF), lambda g: (0, g, 0, 0)),
            pl.BlockSpec((ZROWS, ZROWS), lambda g: (0, 0)),
        ],
        out_specs=pl.BlockSpec((NY, ZG * ROWS, HALF), lambda g: (0, g, 0)),
        out_shape=jax.ShapeDtypeStruct((NY, NZ * ROWS, HALF), BF),
        cost_estimate=pl.CostEstimate(
            flops=2 * NZ // ZG * ZROWS * ZROWS * HALF,
            bytes_accessed=10 * NZ * XROWS * HALF,
            transcendentals=0,
        ),
        name="sum_over_x",
    )(parts, jnp.asarray(TO_Y, BF))


def project_kernel(core, mine, other, perm, hidden, cot_mine, cot_other, keys, grad, acc_mine, acc_other):
    z = pl.program_id(0)

    @pl.when(z == 0)
    def _():
        acc_mine[...] = jnp.zeros_like(acc_mine)
        acc_other[...] = jnp.zeros_like(acc_other)

    w_mine = jnp.dot(
        perm[...], mine[...].reshape(ZROWS, HALF), preferred_element_type=F32
    ).astype(BF)
    w_other = jnp.dot(
        perm[...], other[...].reshape(ZROWS, HALF), preferred_element_type=F32
    ).astype(BF)
    acc_mine[...] += jnp.dot(hidden[...], w_mine, preferred_element_type=F32)
    acc_other[...] += jnp.dot(hidden[...], w_other, preferred_element_type=F32)
    dims = (((1,), (1,)), ((), ()))
    g = lax.dot_general(cot_mine[...], w_mine, dims, preferred_element_type=F32)
    g += lax.dot_general(cot_other[...], w_other, dims, preferred_element_type=F32)
    grad[...] = g.astype(BF)

    @pl.when((z == NZ - 1) & (core[0] == 0))
    def _():
        keys[:, :HALF] = acc_mine[...].astype(BF)
        keys[:, HALF:] = acc_other[...].astype(BF)

    @pl.when((z == NZ - 1) & (core[0] == 1))
    def _():
        keys[:, :HALF] = acc_other[...].astype(BF)
        keys[:, HALF:] = acc_mine[...].astype(BF)


def project(core, mine, other, hidden, cotangent):
    tokens, width = hidden.shape
    block = pl.BlockSpec((NY, 1, NX * ROWS, HALF), lambda z, core: (0, z, 0, 0))
    return pl.pallas_call(
        project_kernel,
        grid_spec=pltpu.PrefetchScalarGridSpec(
            num_scalar_prefetch=1,
            grid=(NZ,),
            in_specs=[
                block,
                block,
                pl.BlockSpec((ZROWS, ZROWS), lambda z, core: (0, 0)),
                pl.BlockSpec((tokens, ZROWS), lambda z, core: (0, z)),
                pl.BlockSpec((tokens, HALF), lambda z, core: (0, core[0])),
                pl.BlockSpec((tokens, HALF), lambda z, core: (0, 1 - core[0])),
            ],
            out_specs=[
                pl.BlockSpec((tokens, 2 * HALF), lambda z, core: (0, 0)),
                pl.BlockSpec((tokens, ZROWS), lambda z, core: (0, z)),
            ],
            scratch_shapes=[pltpu.VMEM((tokens, HALF), F32), pltpu.VMEM((tokens, HALF), F32)],
        ),
        out_shape=[
            jax.ShapeDtypeStruct((tokens, 2 * HALF), BF),
            jax.ShapeDtypeStruct((tokens, width), BF),
        ],
        cost_estimate=pl.CostEstimate(
            flops=4 * width * HALF * (2 * tokens + ZROWS),
            bytes_accessed=4 * tokens * width + 4 * width * HALF,
            transcendentals=0,
        ),
        name="project",
    )(core, mine, other, jnp.asarray(TO_NATURAL, BF), hidden, cotangent, cotangent)


def to_all(piece, axis, count):
    return lax.all_to_all(
        jnp.broadcast_to(piece[None], (count, *piece.shape)), axis, split_axis=0, concat_axis=0, tiled=True
    )


def on_device(hidden, cotangent, quant_weight, scales):
    core = lax.axis_index("c").astype(jnp.int32).reshape(1)
    swap = [(0, 1), (1, 0)]
    factor = 1.0 / math.sqrt(hidden.shape[0] * NZ * NX * NY * NC)

    other_hidden = lax.ppermute(hidden, "c", swap)
    other_cot = lax.ppermute(cotangent, "c", swap)

    shard = (quant_weight.astype(F32) * scales.astype(F32)[:, None]).astype(BF)
    over_z = to_all(shard, "z", NZ)
    over_x = to_all(over_z, "x", NX)
    mine = lax.all_gather(
        over_x.transpose(1, 0, 2, 3).reshape(NZ * NX * ROWS, HALF), Y, axis=0, tiled=True
    ).reshape(NY, NZ, NX * ROWS, HALF)

    term = chip_term(core, hidden, other_hidden, cotangent, other_cot)
    over_x = lax.all_to_all(term, "x", split_axis=0, concat_axis=0, tiled=True)
    sum_x = sum_over_x(over_x)
    over_y = lax.all_to_all(sum_x, Y, split_axis=0, concat_axis=0, tiled=True)
    sum_y = over_y.astype(F32).sum(0).astype(BF).reshape(NZ, ROWS, HALF)
    over_z = lax.all_to_all(sum_y, "z", split_axis=0, concat_axis=0, tiled=True)
    weight_grad = over_z.astype(F32).sum(0) * factor

    other = lax.ppermute(mine, "c", swap)
    keys, grad_input = project(core, mine, other, hidden, cotangent)
    return keys, grad_input, weight_grad


def solution(mesh):
    fine = Mesh(mesh.devices.reshape(NZ, NX, NYH, NYL, NC), ("z", "x", "yh", "yl", "c"))
    node, local = ("z", "x", "yh"), ("yl", "c")
    return jax.shard_map(
        on_device,
        mesh=fine,
        in_specs=(P(node + local, None), P(node + local, None), P(node, local), P(node)),
        out_specs=(P(node + local, None), P(node + local, None), P(node, local)),
        check_vma=False,
    )
```

```python
import math

import jax
import jax.numpy as jnp
import numpy as np
from jax import lax
from jax.experimental import pallas as pl
from jax.experimental.pallas import tpu as pltpu
from jax.sharding import Mesh
from jax.sharding import PartitionSpec as P

NZ, NX, NYH, NYL, NC = 12, 4, 2, 4, 2
NY = NYH * NYL
Y = ("yh", "yl")
ROWS = 12
HALF = 256
ZROWS = NX * NY * ROWS
XROWS = NY * ROWS

BF = jnp.bfloat16
F32 = jnp.float32

_x, _yh, _i, _yl = np.meshgrid(
    np.arange(NX), np.arange(NYH), np.arange(ROWS), np.arange(NYL), indexing="ij"
)
_natural = (((_x * NYH + _yh) * ROWS + _i) * NYL + _yl).ravel()
TO_SEND = np.zeros((NX, ZROWS, ZROWS), np.float32)
FROM_HELD = np.zeros((NX, ZROWS, ZROWS), np.float32)
for _me in range(NX):
    _rest = (_yh * NYL + _yl) * ROWS + _i
    TO_SEND[_me, ((_x - _me) % NX * XROWS + _rest).ravel(), _natural] = 1
    FROM_HELD[_me, _natural, ((_me - _x) % NX * XROWS + _rest).ravel()] = 1
ZG = 4
_z, _y, _i2 = np.meshgrid(np.arange(ZG), np.arange(NY), np.arange(ROWS), indexing="ij")
TO_Y = np.zeros((ZROWS, ZROWS), np.float32)
TO_Y[((_y * ZG + _z) * ROWS + _i2).ravel(), ((_z * NY + _y) * ROWS + _i2).ravel()] = 1
FROM_Y = TO_Y.T
ZSTEP = 3


def term_kernel(place, mine, other, cot_mine, cot_other, perm, *rest):
    *outs, flipped = rest
    tokens = mine.shape[0]

    @pl.when(pl.program_id(0) == 0)
    def _():
        flipped[:, :tokens] = cot_mine[...].T
        flipped[:, tokens:] = cot_other[...].T

    for k in range(ZSTEP):
        cols = slice(k * ZROWS, (k + 1) * ZROWS)
        rows = jnp.concatenate([mine[:, cols], other[:, cols]], axis=0)
        term = jnp.dot(flipped[...], rows, preferred_element_type=F32).astype(BF)
        moved = lax.dot_general(
            perm[0], term, (((1,), (1,)), ((), ())), preferred_element_type=F32
        ).astype(BF)
        for r in range(NX):
            outs[r][k] = moved[r * XROWS : (r + 1) * XROWS]


def chip_term(place, mine, other, cot_mine, cot_other):
    tokens, width = mine.shape
    wide = pl.BlockSpec((tokens, ZSTEP * ZROWS), lambda z, place: (0, z))
    half = pl.BlockSpec((tokens, HALF), lambda z, place: (0, place[0]))
    return pl.pallas_call(
        term_kernel,
        grid_spec=pltpu.PrefetchScalarGridSpec(
            num_scalar_prefetch=1,
            grid=(NZ // ZSTEP,),
            in_specs=[
                wide,
                wide,
                half,
                half,
                pl.BlockSpec((1, ZROWS, ZROWS), lambda z, place: (place[1], 0, 0)),
            ],
            out_specs=[pl.BlockSpec((ZSTEP, XROWS, HALF), lambda z, place: (z, 0, 0))] * NX,
            scratch_shapes=[pltpu.VMEM((HALF, 2 * tokens), BF)],
        ),
        out_shape=[jax.ShapeDtypeStruct((NZ, XROWS, HALF), BF)] * NX,
        compiler_params=pltpu.CompilerParams(vmem_limit_bytes=56 * 2**20),
        cost_estimate=pl.CostEstimate(
            flops=2 * width * HALF * (2 * tokens + ZROWS),
            bytes_accessed=4 * tokens * width + 2 * width * HALF,
            transcendentals=0,
        ),
        name="chip_term",
    )(place, mine, other, cot_mine, cot_other, jnp.asarray(TO_SEND, BF))


def sum_kernel(*refs):
    *parts, perm, _, out = refs
    total = parts[0][...].astype(F32)
    for part in parts[1:]:
        total += part[...].astype(F32)
    rows = total.astype(BF).reshape(ZROWS, HALF)
    moved = jnp.dot(perm[...], rows, preferred_element_type=F32)
    out[...] = moved.astype(BF).reshape(out.shape)


def sum_over_x(parts, first):
    return pl.pallas_call(
        sum_kernel,
        grid=(NZ // ZG,),
        in_specs=[pl.BlockSpec((ZG, XROWS, HALF), lambda g: (g, 0, 0))] * NX
        + [pl.BlockSpec((ZROWS, ZROWS), lambda g: (0, 0)), pl.BlockSpec(memory_space=pl.ANY)],
        out_specs=pl.BlockSpec((NY, ZG * ROWS, HALF), lambda g: (0, g, 0)),
        out_shape=jax.ShapeDtypeStruct((NY, NZ * ROWS, HALF), BF),
        compiler_params=pltpu.CompilerParams(vmem_limit_bytes=12 * 2**20),
        cost_estimate=pl.CostEstimate(
            flops=2 * NZ // ZG * ZROWS * ZROWS * HALF,
            bytes_accessed=10 * NZ * XROWS * HALF,
            transcendentals=0,
        ),
        name="sum_over_x",
    )(*parts, jnp.asarray(TO_Y, BF), first)


def regroup_kernel(parts, perm, out):
    rows = parts[...].reshape(ZROWS, HALF)
    out[...] = jnp.dot(perm[...], rows, preferred_element_type=F32).astype(BF).reshape(out.shape)


def regroup(parts):
    return pl.pallas_call(
        regroup_kernel,
        grid=(NZ // ZG,),
        in_specs=[
            pl.BlockSpec((NY, ZG * ROWS, HALF), lambda g: (0, g, 0)),
            pl.BlockSpec((ZROWS, ZROWS), lambda g: (0, 0)),
        ],
        out_specs=pl.BlockSpec((ZG, XROWS, HALF), lambda g: (g, 0, 0)),
        out_shape=jax.ShapeDtypeStruct((NZ, XROWS, HALF), BF),
        compiler_params=pltpu.CompilerParams(vmem_limit_bytes=12 * 2**20),
        cost_estimate=pl.CostEstimate(
            flops=2 * NZ // ZG * ZROWS * ZROWS * HALF,
            bytes_accessed=4 * NZ * XROWS * HALF,
            transcendentals=0,
        ),
        name="regroup",
    )(parts, jnp.asarray(FROM_Y, BF))


def project_kernel(place, *refs):
    *blocks, perm, hidden, cot_mine, cot_other, keys, grad, acc, cot = refs
    step = pl.program_id(0)

    @pl.when(step == 0)
    def _():
        cot[:, :HALF] = cot_mine[...]
        cot[:, HALF:] = cot_other[...]
        acc[...] = jnp.zeros_like(acc)

    total = acc[...]
    for k in range(ZSTEP):
        cols = slice(k * ZROWS, (k + 1) * ZROWS)
        held = jnp.concatenate(
            [jnp.concatenate([b[k] for b in blocks[s : s + NX]], axis=0) for s in (0, NX)], axis=1
        )
        weight = jnp.dot(perm[0], held, preferred_element_type=F32).astype(BF)
        total += jnp.dot(hidden[:, cols], weight, preferred_element_type=F32)
        grad[:, cols] = lax.dot_general(
            cot[...], weight, (((1,), (1,)), ((), ())), preferred_element_type=F32
        ).astype(BF)
    acc[...] = total

    @pl.when((step == NZ // ZSTEP - 1) & (place[0] == 0))
    def _():
        keys[...] = acc[...].astype(BF)

    @pl.when((step == NZ // ZSTEP - 1) & (place[0] == 1))
    def _():
        keys[:, :HALF] = acc[:, HALF:].astype(BF)
        keys[:, HALF:] = acc[:, :HALF].astype(BF)


def project(place, mine, other, hidden, cotangent):
    tokens, width = hidden.shape
    block = pl.BlockSpec((ZSTEP, XROWS, HALF), lambda z, place: (z, 0, 0))
    wide = pl.BlockSpec((tokens, ZSTEP * ZROWS), lambda z, place: (0, z))
    return pl.pallas_call(
        project_kernel,
        grid_spec=pltpu.PrefetchScalarGridSpec(
            num_scalar_prefetch=1,
            grid=(NZ // ZSTEP,),
            in_specs=[block] * (2 * NX)
            + [
                pl.BlockSpec((1, ZROWS, ZROWS), lambda z, place: (place[1], 0, 0)),
                wide,
                pl.BlockSpec((tokens, HALF), lambda z, place: (0, place[0])),
                pl.BlockSpec((tokens, HALF), lambda z, place: (0, 1 - place[0])),
            ],
            out_specs=[pl.BlockSpec((tokens, 2 * HALF), lambda z, place: (0, 0)), wide],
            scratch_shapes=[
                pltpu.VMEM((tokens, 2 * HALF), F32),
                pltpu.VMEM((tokens, 2 * HALF), BF),
            ],
        ),
        out_shape=[
            jax.ShapeDtypeStruct((tokens, 2 * HALF), BF),
            jax.ShapeDtypeStruct((tokens, width), BF),
        ],
        compiler_params=pltpu.CompilerParams(vmem_limit_bytes=56 * 2**20),
        cost_estimate=pl.CostEstimate(
            flops=4 * width * HALF * (2 * tokens + ZROWS),
            bytes_accessed=4 * tokens * width + 4 * width * HALF,
            transcendentals=0,
        ),
        name="project",
    )(place, *mine, *other, jnp.asarray(FROM_HELD, BF), hidden, cotangent, cotangent)


def to_all(piece, axis, count):
    copies = jnp.broadcast_to(piece[None], (count, *piece.shape))
    return lax.all_to_all(copies, axis, split_axis=0, concat_axis=0, tiled=True)


def shift(piece, r):
    return lax.ppermute(piece, "x", [(k, (k + r) % NX) for k in range(NX)])


def swap(piece):
    return lax.ppermute(piece, "c", [(0, 1), (1, 0)])


def on_device(hidden, cotangent, quant_weight, scales):
    place = jnp.stack([lax.axis_index("c"), lax.axis_index("x")]).astype(jnp.int32)
    factor = 1.0 / math.sqrt(hidden.shape[0] * NZ * NX * NY * NC)

    other_hidden = swap(hidden)
    other_cot = swap(cotangent)

    shard = (quant_weight.astype(F32) * scales.astype(F32)[:, None]).astype(BF)
    w_z = to_all(shard, "z", NZ)

    terms = chip_term(place, hidden, other_hidden, cotangent, other_cot)
    w_z, terms = lax.optimization_barrier((w_z, terms))
    t_x = [terms[0]] + [shift(terms[r], r) for r in range(1, NX)]
    w_y = regroup(to_all(w_z.reshape(NZ * ROWS, HALF), Y, NY))

    mine = [w_y] + [shift(w_y, r) for r in range(1, NX)]
    other = [swap(piece) for piece in mine]
    sum_x = sum_over_x(t_x, w_y)
    t_y = lax.all_to_all(sum_x, Y, split_axis=0, concat_axis=0, tiled=True)
    sum_y = t_y.astype(F32).sum(0).astype(BF).reshape(NZ, ROWS, HALF)
    t_z = lax.all_to_all(sum_y, "z", split_axis=0, concat_axis=0, tiled=True)
    weight_grad = t_z.astype(F32).sum(0) * factor
    keys, grad_input = project(place, mine, other, hidden, cotangent)
    return keys, grad_input, weight_grad


def solution(mesh):
    fine = Mesh(mesh.devices.reshape(NZ, NX, NYH, NYL, NC), ("z", "x", "yh", "yl", "c"))
    node, local = ("z", "x", "yh"), ("yl", "c")
    return jax.shard_map(
        on_device,
        mesh=fine,
        in_specs=(P(node + local, None), P(node + local, None), P(node, local), P(node)),
        out_specs=(P(node + local, None), P(node + local, None), P(node, local)),
        check_vma=False,
    )
```

```python
import math

import jax
import jax.numpy as jnp
import numpy as np
from jax import lax
from jax.experimental import pallas as pl
from jax.experimental.pallas import tpu as pltpu
from jax.sharding import Mesh
from jax.sharding import PartitionSpec as P

NZ, NX, NYH, NYL, NC = 12, 4, 2, 4, 2
NY = NYH * NYL
Y = ("yh", "yl")
ROWS = 12
HALF = 256
ZROWS = NX * NY * ROWS
XROWS = NY * ROWS

BF = jnp.bfloat16
F32 = jnp.float32

ZG = 4
_z, _yh, _i, _yl = np.meshgrid(
    np.arange(ZG), np.arange(NYH), np.arange(ROWS), np.arange(NYL), indexing="ij"
)
BY_DEVICE = np.zeros((ZG * XROWS, ZG * XROWS), np.float32)
BY_DEVICE[(((_yh * NYL + _yl) * ZG + _z) * ROWS + _i).ravel(), np.arange(ZG * XROWS)] = 1
IN_ORDER = BY_DEVICE.T
ZSTEP = 3


def term_kernel(place, mine, other, cot_mine, cot_other, *rest):
    *outs, flipped, held = rest
    tokens = mine.shape[0]

    @pl.when(pl.program_id(0) == 0)
    def _():
        flipped[:, :tokens] = cot_mine[...].T
        flipped[:, tokens:] = cot_other[...].T

    for k in range(ZSTEP):
        cols = slice(k * ZROWS, (k + 1) * ZROWS)
        rows = jnp.concatenate([mine[:, cols], other[:, cols]], axis=0)
        term = jnp.dot(flipped[...], rows, preferred_element_type=F32).astype(BF)
        held[k] = term.T
        for r in range(NX):
            x = lax.rem(place[1] + r, NX)
            outs[r][k] = held[k, pl.ds(pl.multiple_of(x * XROWS, XROWS), XROWS)]


def chip_term(place, mine, other, cot_mine, cot_other):
    tokens, width = mine.shape
    wide = pl.BlockSpec((tokens, ZSTEP * ZROWS), lambda z, place: (0, z))
    half = pl.BlockSpec((tokens, HALF), lambda z, place: (0, place[0]))
    return pl.pallas_call(
        term_kernel,
        grid_spec=pltpu.PrefetchScalarGridSpec(
            num_scalar_prefetch=1,
            grid=(NZ // ZSTEP,),
            in_specs=[wide, wide, half, half],
            out_specs=[pl.BlockSpec((ZSTEP, XROWS, HALF), lambda z, place: (z, 0, 0))] * NX,
            scratch_shapes=[
                pltpu.VMEM((HALF, 2 * tokens), BF),
                pltpu.VMEM((ZSTEP, ZROWS, HALF), BF),
            ],
        ),
        out_shape=[jax.ShapeDtypeStruct((NZ, XROWS, HALF), BF)] * NX,
        compiler_params=pltpu.CompilerParams(vmem_limit_bytes=56 * 2**20),
        cost_estimate=pl.CostEstimate(
            flops=4 * width * HALF * tokens,
            bytes_accessed=4 * tokens * width + 2 * width * HALF,
            transcendentals=0,
        ),
        name="chip_term",
    )(place, mine, other, cot_mine, cot_other)


def sum_kernel(*refs):
    *parts, perm, out = refs
    total = parts[0][...].astype(F32)
    for part in parts[1:]:
        total += part[...].astype(F32)
    rows = total.astype(BF).reshape(ZROWS, HALF)
    moved = jnp.dot(perm[...], rows, preferred_element_type=F32)
    out[...] = moved.astype(BF).reshape(out.shape)


def sum_over_x(parts):
    return pl.pallas_call(
        sum_kernel,
        grid=(NZ // ZG,),
        in_specs=[pl.BlockSpec((ZG, XROWS, HALF), lambda g: (g, 0, 0))] * NX
        + [pl.BlockSpec((ZROWS, ZROWS), lambda g: (0, 0))],
        out_specs=pl.BlockSpec((NY, ZG * ROWS, HALF), lambda g: (0, g, 0)),
        out_shape=jax.ShapeDtypeStruct((NY, NZ * ROWS, HALF), BF),
        compiler_params=pltpu.CompilerParams(vmem_limit_bytes=12 * 2**20),
        cost_estimate=pl.CostEstimate(
            flops=200 * NZ // ZG * ZROWS * ZROWS * HALF,
            bytes_accessed=10 * NZ * XROWS * HALF,
            transcendentals=0,
        ),
        name="sum_over_x",
    )(*parts, jnp.asarray(BY_DEVICE, BF))


def regroup_kernel(parts, perm, _, out):
    rows = parts[...].reshape(ZROWS, HALF)
    out[...] = jnp.dot(perm[...], rows, preferred_element_type=F32).astype(BF).reshape(out.shape)


def regroup(parts, first):
    return pl.pallas_call(
        regroup_kernel,
        grid=(NZ // ZG,),
        in_specs=[
            pl.BlockSpec((NY, ZG * ROWS, HALF), lambda g: (0, g, 0)),
            pl.BlockSpec((ZROWS, ZROWS), lambda g: (0, 0)),
            pl.BlockSpec(memory_space=pl.ANY),
        ],
        out_specs=pl.BlockSpec((ZG, XROWS, HALF), lambda g: (g, 0, 0)),
        out_shape=jax.ShapeDtypeStruct((NZ, XROWS, HALF), BF),
        compiler_params=pltpu.CompilerParams(vmem_limit_bytes=12 * 2**20),
        cost_estimate=pl.CostEstimate(
            flops=2 * NZ // ZG * ZROWS * ZROWS * HALF,
            bytes_accessed=4 * NZ * XROWS * HALF,
            transcendentals=0,
        ),
        name="regroup",
    )(parts, jnp.asarray(IN_ORDER, BF), first)


def project_kernel(place, *refs):
    *blocks, hidden, cot_mine, cot_other, keys, grad, acc, cot, held = refs
    step = pl.program_id(0)

    @pl.when(step == 0)
    def _():
        cot[:, :HALF] = cot_mine[...]
        cot[:, HALF:] = cot_other[...]
        acc[...] = jnp.zeros_like(acc)

    total = acc[...]
    for k in range(ZSTEP):
        for r in range(NX):
            x = lax.rem(place[1] + NX - r, NX)
            rows = pl.ds(pl.multiple_of(x * XROWS, XROWS), XROWS)
            held[k, rows, :HALF] = blocks[r][k]
            held[k, rows, HALF:] = blocks[NX + r][k]
        weight = held[k]
        cols = slice(k * ZROWS, (k + 1) * ZROWS)
        total += jnp.dot(hidden[:, cols], weight, preferred_element_type=F32)
        grad[:, cols] = lax.dot_general(
            cot[...], weight, (((1,), (1,)), ((), ())), preferred_element_type=F32
        ).astype(BF)
    acc[...] = total

    @pl.when((step == NZ // ZSTEP - 1) & (place[0] == 0))
    def _():
        keys[...] = acc[...].astype(BF)

    @pl.when((step == NZ // ZSTEP - 1) & (place[0] == 1))
    def _():
        keys[:, :HALF] = acc[:, HALF:].astype(BF)
        keys[:, HALF:] = acc[:, :HALF].astype(BF)


def project(place, mine, other, hidden, cotangent):
    tokens, width = hidden.shape
    block = pl.BlockSpec((ZSTEP, XROWS, HALF), lambda z, place: (z, 0, 0))
    wide = pl.BlockSpec((tokens, ZSTEP * ZROWS), lambda z, place: (0, z))
    return pl.pallas_call(
        project_kernel,
        grid_spec=pltpu.PrefetchScalarGridSpec(
            num_scalar_prefetch=1,
            grid=(NZ // ZSTEP,),
            in_specs=[block] * (2 * NX)
            + [
                wide,
                pl.BlockSpec((tokens, HALF), lambda z, place: (0, place[0])),
                pl.BlockSpec((tokens, HALF), lambda z, place: (0, 1 - place[0])),
            ],
            out_specs=[
                pl.BlockSpec((tokens, 2 * HALF), lambda z, place: (0, 0)),
                wide,
            ],
            scratch_shapes=[
                pltpu.VMEM((tokens, 2 * HALF), F32),
                pltpu.VMEM((tokens, 2 * HALF), BF),
                pltpu.VMEM((ZSTEP, ZROWS, 2 * HALF), BF),
            ],
        ),
        out_shape=[
            jax.ShapeDtypeStruct((tokens, 2 * HALF), BF),
            jax.ShapeDtypeStruct((tokens, width), BF),
        ],
        compiler_params=pltpu.CompilerParams(vmem_limit_bytes=16 * 2**20),
        cost_estimate=pl.CostEstimate(
            flops=8 * width * HALF * tokens,
            bytes_accessed=4 * tokens * width + 4 * width * HALF,
            transcendentals=0,
        ),
        name="project",
    )(place, *mine, *other, hidden, cotangent, cotangent)


def shard_kernel(values, scales, out):
    rows = lax.broadcasted_iota(jnp.int32, (ROWS, ROWS), 0)
    cols = lax.broadcasted_iota(jnp.int32, (ROWS, ROWS), 1)
    line = jnp.broadcast_to(scales[...].astype(F32), (ROWS, ROWS))
    column = jnp.sum(jnp.where(rows == cols, line, 0.0), axis=1, keepdims=True)
    shard = (values[...].astype(F32) * column).astype(BF)
    for z in range(NZ):
        out[z] = shard


def scaled_copies(values, scales):
    return pl.pallas_call(
        shard_kernel,
        out_shape=jax.ShapeDtypeStruct((NZ, ROWS, HALF), BF),
        compiler_params=pltpu.CompilerParams(vmem_limit_bytes=4 * 2**20),
        name="scaled_copies",
    )(values, scales.reshape(1, ROWS))


def to_all(piece, axis, count):
    copies = jnp.broadcast_to(piece[None], (count, *piece.shape))
    return lax.all_to_all(copies, axis, split_axis=0, concat_axis=0, tiled=True)


def shift(piece, r):
    return lax.ppermute(piece, "x", [(k, (k + r) % NX) for k in range(NX)])


def swap(piece):
    return lax.ppermute(piece, "c", [(0, 1), (1, 0)])


def on_device(hidden, cotangent, quant_weight, scales):
    place = jnp.stack([lax.axis_index("c"), lax.axis_index("x")]).astype(jnp.int32)
    factor = 1.0 / math.sqrt(hidden.shape[0] * NZ * NX * NY * NC)

    other_hidden = swap(hidden)
    other_cot = swap(cotangent)

    copies = scaled_copies(quant_weight, scales)
    w_z = lax.all_to_all(copies, "z", split_axis=0, concat_axis=0, tiled=True)

    terms = chip_term(place, hidden, other_hidden, cotangent, other_cot)
    w_z, terms = lax.optimization_barrier((w_z, terms))
    t_x = [terms[0]] + [shift(terms[r], r) for r in range(1, NX)]
    sum_x = sum_over_x(t_x)
    w_y = regroup(to_all(w_z.reshape(NZ * ROWS, HALF), Y, NY), sum_x)

    mine = [w_y] + [shift(w_y, r) for r in range(1, NX)]
    t_y = lax.all_to_all(sum_x, Y, split_axis=0, concat_axis=0, tiled=True)
    sum_y = t_y.astype(F32).sum(0).astype(BF).reshape(NZ, ROWS, HALF)
    t_z = lax.all_to_all(sum_y, "z", split_axis=0, concat_axis=0, tiled=True)
    late = [lax.optimization_barrier((piece, t_z))[0] for piece in mine[1:]]
    other = [swap(piece) for piece in [w_y] + late]
    weight_grad = t_z.astype(F32).sum(0) * factor
    keys, grad_input = project(place, mine, other, hidden, cotangent)
    return keys, grad_input, weight_grad


def solution(mesh):
    fine = Mesh(mesh.devices.reshape(NZ, NX, NYH, NYL, NC), ("z", "x", "yh", "yl", "c"))
    node, local = ("z", "x", "yh"), ("yl", "c")
    return jax.shard_map(
        on_device,
        mesh=fine,
        in_specs=(P(node + local, None), P(node + local, None), P(node, local), P(node)),
        out_specs=(P(node + local, None), P(node + local, None), P(node, local)),
        check_vma=False,
    )
```

```python
import math

import jax
import jax.numpy as jnp
import numpy as np
from jax import lax
from jax.experimental import pallas as pl
from jax.experimental.pallas import tpu as pltpu
from jax.sharding import Mesh
from jax.sharding import PartitionSpec as P

NZ, NX, NYH, NYL, NC = 12, 4, 2, 4, 2
NY = NYH * NYL
Y = ("yh", "yl")
ROWS = 12
HALF = 256
ZROWS = NX * NY * ROWS
XROWS = NY * ROWS
WIDE = NZ * XROWS

BF = jnp.bfloat16
F32 = jnp.float32

ZG = 4
_z, _yh, _i, _yl = np.meshgrid(
    np.arange(ZG), np.arange(NYH), np.arange(ROWS), np.arange(NYL), indexing="ij"
)
BY_DEVICE = np.zeros((ZG * XROWS, ZG * XROWS), np.float32)
BY_DEVICE[(((_yh * NYL + _yl) * ZG + _z) * ROWS + _i).ravel(), np.arange(ZG * XROWS)] = 1
IN_ORDER = BY_DEVICE.T
ZSTEP = 3


def pack_kernel(place, hidden, cot, *rest):
    *outs, cut = rest
    for g in range(NZ // ZG):
        for x in range(NX):
            starts = [z * ZROWS + x * XROWS for z in range(g * ZG, (g + 1) * ZG)]
            cut[x, :, g * ZG * XROWS : (g + 1) * ZG * XROWS] = jnp.concatenate(
                [hidden[:, start : start + XROWS] for start in starts], axis=1
            )
    for r in range(NX):
        outs[r][:, :WIDE] = cut[lax.rem(place[1] + r, NX)]
        outs[r][:, WIDE:] = cot[...]


def pack(place, hidden, cotangent):
    tokens, width = hidden.shape
    whole = pl.BlockSpec((tokens, WIDE + 2 * HALF), lambda k, place: (0, 0))
    return pl.pallas_call(
        pack_kernel,
        grid_spec=pltpu.PrefetchScalarGridSpec(
            num_scalar_prefetch=1,
            grid=(1,),
            in_specs=[
                pl.BlockSpec((tokens, width), lambda k, place: (0, 0)),
                pl.BlockSpec((tokens, 2 * HALF), lambda k, place: (0, 0)),
            ],
            out_specs=[whole] * NX,
            scratch_shapes=[pltpu.VMEM((NX, tokens, WIDE), BF)],
        ),
        out_shape=[jax.ShapeDtypeStruct((tokens, WIDE + 2 * HALF), BF)] * NX,
        compiler_params=pltpu.CompilerParams(vmem_limit_bytes=56 * 2**20),
        cost_estimate=pl.CostEstimate(
            flops=tokens * width, bytes_accessed=4 * tokens * width, transcendentals=0
        ),
        name="pack",
    )(place, hidden, cotangent)


def term_kernel(place, *refs):
    *blocks, perm, out, flipped = refs
    tokens = blocks[0].shape[0]
    half = pl.ds(pl.multiple_of(WIDE + place[0] * HALF, HALF // 2), HALF)
    for b in range(0, len(blocks), 2):
        pair = jnp.concatenate([blocks[b][:, half], blocks[b + 1][:, half]], axis=0)
        flipped[:, b * tokens : (b + 2) * tokens] = pair.T
    for g in range(NZ // ZG):
        cols = slice(g * ZG * XROWS, (g + 1) * ZG * XROWS)
        rows = jnp.concatenate([block[:, cols] for block in blocks], axis=0)
        term = jnp.dot(flipped[...], rows, preferred_element_type=F32).astype(BF)
        moved = lax.dot_general(
            perm[...], term, (((1,), (1,)), ((), ())), preferred_element_type=F32
        ).astype(BF)
        out[:, g * ZG * ROWS : (g + 1) * ZG * ROWS] = moved.reshape(NY, ZG * ROWS, HALF)


def group_term(place, blocks):
    tokens = blocks[0].shape[0]
    whole = pl.BlockSpec(memory_space=pltpu.VMEM)
    return pl.pallas_call(
        term_kernel,
        grid_spec=pltpu.PrefetchScalarGridSpec(
            num_scalar_prefetch=1,
            grid=(1,),
            in_specs=[whole] * len(blocks)
            + [pl.BlockSpec((ZG * XROWS, ZG * XROWS), lambda k, place: (0, 0))],
            out_specs=pl.BlockSpec((NY, NZ * ROWS, HALF), lambda k, place: (0, 0, 0)),
            scratch_shapes=[pltpu.VMEM((HALF, len(blocks) * tokens), BF)],
        ),
        out_shape=jax.ShapeDtypeStruct((NY, NZ * ROWS, HALF), BF),
        compiler_params=pltpu.CompilerParams(vmem_limit_bytes=24 * 2**20),
        cost_estimate=pl.CostEstimate(
            flops=2 * WIDE * HALF * (len(blocks) * tokens + ZG * XROWS),
            bytes_accessed=2 * len(blocks) * tokens * (WIDE + 2 * HALF),
            transcendentals=0,
        ),
        name="group_term",
    )(place, *blocks, jnp.asarray(BY_DEVICE, BF))


def regroup_kernel(parts, perm, out):
    rows = parts[...].reshape(ZROWS, HALF)
    out[...] = jnp.dot(perm[...], rows, preferred_element_type=F32).astype(BF).reshape(out.shape)


def regroup(parts):
    return pl.pallas_call(
        regroup_kernel,
        grid=(NZ // ZG,),
        in_specs=[
            pl.BlockSpec((NY, ZG * ROWS, HALF), lambda g: (0, g, 0)),
            pl.BlockSpec((ZROWS, ZROWS), lambda g: (0, 0)),
        ],
        out_specs=pl.BlockSpec((ZG, XROWS, HALF), lambda g: (g, 0, 0)),
        out_shape=jax.ShapeDtypeStruct((NZ, XROWS, HALF), BF),
        compiler_params=pltpu.CompilerParams(vmem_limit_bytes=12 * 2**20),
        cost_estimate=pl.CostEstimate(
            flops=2 * NZ // ZG * ZROWS * ZROWS * HALF,
            bytes_accessed=4 * NZ * XROWS * HALF,
            transcendentals=0,
        ),
        name="regroup",
    )(parts, jnp.asarray(IN_ORDER, BF))


def project_kernel(place, *refs):
    *blocks, hidden, cot_mine, cot_other, keys, grad, acc, cot, held = refs
    step = pl.program_id(0)

    @pl.when(step == 0)
    def _():
        cot[:, :HALF] = cot_mine[...]
        cot[:, HALF:] = cot_other[...]
        acc[...] = jnp.zeros_like(acc)

    total = acc[...]
    for k in range(ZSTEP):
        for r in range(NX):
            x = lax.rem(place[1] + NX - r, NX)
            rows = pl.ds(pl.multiple_of(x * XROWS, XROWS), XROWS)
            held[k, rows, :HALF] = blocks[r][k]
            held[k, rows, HALF:] = blocks[NX + r][k]
        weight = held[k]
        cols = slice(k * ZROWS, (k + 1) * ZROWS)
        total += jnp.dot(hidden[:, cols], weight, preferred_element_type=F32)
        grad[:, cols] = lax.dot_general(
            cot[...], weight, (((1,), (1,)), ((), ())), preferred_element_type=F32
        ).astype(BF)
    acc[...] = total

    @pl.when((step == NZ // ZSTEP - 1) & (place[0] == 0))
    def _():
        keys[...] = acc[...].astype(BF)

    @pl.when((step == NZ // ZSTEP - 1) & (place[0] == 1))
    def _():
        keys[:, :HALF] = acc[:, HALF:].astype(BF)
        keys[:, HALF:] = acc[:, :HALF].astype(BF)


def project(place, mine, other, hidden, cotangent):
    tokens, width = hidden.shape
    block = pl.BlockSpec((ZSTEP, XROWS, HALF), lambda z, place: (z, 0, 0))
    wide = pl.BlockSpec((tokens, ZSTEP * ZROWS), lambda z, place: (0, z))
    return pl.pallas_call(
        project_kernel,
        grid_spec=pltpu.PrefetchScalarGridSpec(
            num_scalar_prefetch=1,
            grid=(NZ // ZSTEP,),
            in_specs=[block] * (2 * NX)
            + [
                wide,
                pl.BlockSpec((tokens, HALF), lambda z, place: (0, place[0])),
                pl.BlockSpec((tokens, HALF), lambda z, place: (0, 1 - place[0])),
            ],
            out_specs=[
                pl.BlockSpec((tokens, 2 * HALF), lambda z, place: (0, 0)),
                wide,
            ],
            scratch_shapes=[
                pltpu.VMEM((tokens, 2 * HALF), F32),
                pltpu.VMEM((tokens, 2 * HALF), BF),
                pltpu.VMEM((ZSTEP, ZROWS, 2 * HALF), BF),
            ],
        ),
        out_shape=[
            jax.ShapeDtypeStruct((tokens, 2 * HALF), BF),
            jax.ShapeDtypeStruct((tokens, width), BF),
        ],
        compiler_params=pltpu.CompilerParams(vmem_limit_bytes=16 * 2**20),
        cost_estimate=pl.CostEstimate(
            flops=8 * width * HALF * tokens,
            bytes_accessed=4 * tokens * width + 4 * width * HALF,
            transcendentals=0,
        ),
        name="project",
    )(place, *mine, *other, hidden, cotangent, cotangent)


def shard_kernel(values, scales, out):
    rows = lax.broadcasted_iota(jnp.int32, (ROWS, ROWS), 0)
    cols = lax.broadcasted_iota(jnp.int32, (ROWS, ROWS), 1)
    line = jnp.broadcast_to(scales[...].astype(F32), (ROWS, ROWS))
    column = jnp.sum(jnp.where(rows == cols, line, 0.0), axis=1, keepdims=True)
    shard = (values[...].astype(F32) * column).astype(BF)
    for z in range(NZ):
        out[z] = shard


def scaled_copies(values, scales):
    return pl.pallas_call(
        shard_kernel,
        out_shape=jax.ShapeDtypeStruct((NZ, ROWS, HALF), BF),
        compiler_params=pltpu.CompilerParams(vmem_limit_bytes=4 * 2**20),
        name="scaled_copies",
    )(values, scales.reshape(1, ROWS))


def to_all(piece, axis, count):
    copies = jnp.broadcast_to(piece[None], (count, *piece.shape))
    return lax.all_to_all(copies, axis, split_axis=0, concat_axis=0, tiled=True)


def shift(piece, r):
    return lax.ppermute(piece, "x", [(k, (k + r) % NX) for k in range(NX)])


def swap(piece):
    return lax.ppermute(piece, "c", [(0, 1), (1, 0)])


def on_device(hidden, cotangent, quant_weight, scales):
    place = jnp.stack([lax.axis_index("c"), lax.axis_index("x")]).astype(jnp.int32)
    factor = 1.0 / math.sqrt(hidden.shape[0] * NZ * NX * NY * NC)

    copies = scaled_copies(quant_weight, scales)
    w_z = lax.all_to_all(copies, "z", split_axis=0, concat_axis=0, tiled=True)

    packed = pack(place, hidden, cotangent)
    held = [packed[0]] + [shift(packed[r], r) for r in (1, 3, 2)]
    term = group_term(place, held + [swap(piece) for piece in held])

    w_y = regroup(to_all(w_z.reshape(NZ * ROWS, HALF), Y, NY))
    mine = [w_y] + [shift(w_y, r) for r in range(1, NX)]
    other = [swap(piece) for piece in mine]

    t_y = lax.all_to_all(term, Y, split_axis=0, concat_axis=0, tiled=True)
    sum_y = t_y.astype(F32).sum(0).astype(BF).reshape(NZ, ROWS, HALF)
    t_z = lax.all_to_all(sum_y, "z", split_axis=0, concat_axis=0, tiled=True)
    weight_grad = t_z.astype(F32).sum(0) * factor
    keys, grad_input = project(place, mine, other, hidden, cotangent)
    return keys, grad_input, weight_grad


def solution(mesh):
    fine = Mesh(mesh.devices.reshape(NZ, NX, NYH, NYL, NC), ("z", "x", "yh", "yl", "c"))
    node, local = ("z", "x", "yh"), ("yl", "c")
    return jax.shard_map(
        on_device,
        mesh=fine,
        in_specs=(P(node + local, None), P(node + local, None), P(node, local), P(node)),
        out_specs=(P(node + local, None), P(node + local, None), P(node, local)),
        check_vma=False,
    )
```

```python
import math

import jax
import jax.numpy as jnp
import numpy as np
from jax import lax
from jax.experimental import pallas as pl
from jax.experimental.pallas import tpu as pltpu
from jax.sharding import Mesh
from jax.sharding import PartitionSpec as P

NZ, NX, NYH, NYL, NC = 12, 4, 2, 4, 2
NY = NYH * NYL
Y = ("yh", "yl")
ROWS = 12
HALF = 256
ZROWS = NX * NY * ROWS
XROWS = NY * ROWS
WIDE = NZ * XROWS

BF = jnp.bfloat16
F32 = jnp.float32

ZG = 4
_z, _yh, _i, _yl = np.meshgrid(
    np.arange(ZG), np.arange(NYH), np.arange(ROWS), np.arange(NYL), indexing="ij"
)
BY_DEVICE = np.zeros((ZG * XROWS, ZG * XROWS), np.float32)
BY_DEVICE[(((_yh * NYL + _yl) * ZG + _z) * ROWS + _i).ravel(), np.arange(ZG * XROWS)] = 1
IN_ORDER = BY_DEVICE.T
ZSTEP = 3


def pack_kernel(place, hidden, cot, *rest):
    *outs, cut = rest
    for g in range(NZ // ZG):
        for x in range(NX):
            starts = [z * ZROWS + x * XROWS for z in range(g * ZG, (g + 1) * ZG)]
            cut[x, :, g * ZG * XROWS : (g + 1) * ZG * XROWS] = jnp.concatenate(
                [hidden[:, start : start + XROWS] for start in starts], axis=1
            )
    for r in range(NX):
        outs[r][:, :WIDE] = cut[lax.rem(place[1] + r, NX)]
        outs[r][:, WIDE:] = cot[...]


def pack(place, hidden, cotangent):
    tokens, width = hidden.shape
    step = tokens // 2
    whole = pl.BlockSpec((step, WIDE + 2 * HALF), lambda k, place: (k, 0))
    return pl.pallas_call(
        pack_kernel,
        grid_spec=pltpu.PrefetchScalarGridSpec(
            num_scalar_prefetch=1,
            grid=(2,),
            in_specs=[
                pl.BlockSpec((step, width), lambda k, place: (k, 0)),
                pl.BlockSpec((step, 2 * HALF), lambda k, place: (k, 0)),
            ],
            out_specs=[whole] * NX,
            scratch_shapes=[pltpu.VMEM((NX, step, WIDE), BF)],
        ),
        out_shape=[jax.ShapeDtypeStruct((tokens, WIDE + 2 * HALF), BF)] * NX,
        compiler_params=pltpu.CompilerParams(vmem_limit_bytes=56 * 2**20),
        cost_estimate=pl.CostEstimate(
            flops=tokens * width, bytes_accessed=4 * tokens * width, transcendentals=0
        ),
        name="pack",
    )(place, hidden, cotangent)


def term_kernel(place, *refs):
    *blocks, perm, out, flipped = refs
    tokens = blocks[0].shape[0]
    half = pl.ds(pl.multiple_of(WIDE + place[0] * HALF, HALF // 2), HALF)
    for b in range(0, len(blocks), 2):
        pair = jnp.concatenate([blocks[b][:, half], blocks[b + 1][:, half]], axis=0)
        flipped[:, b * tokens : (b + 2) * tokens] = pair.T
    for g in range(NZ // ZG):
        cols = slice(g * ZG * XROWS, (g + 1) * ZG * XROWS)
        rows = jnp.concatenate([block[:, cols] for block in blocks], axis=0)
        term = jnp.dot(flipped[...], rows, preferred_element_type=F32).astype(BF)
        moved = lax.dot_general(
            perm[...], term, (((1,), (1,)), ((), ())), preferred_element_type=F32
        ).astype(BF)
        out[:, g * ZG * ROWS : (g + 1) * ZG * ROWS] = moved.reshape(NY, ZG * ROWS, HALF)


def group_term(place, blocks):
    tokens = blocks[0].shape[0]
    whole = pl.BlockSpec(memory_space=pltpu.VMEM)
    return pl.pallas_call(
        term_kernel,
        grid_spec=pltpu.PrefetchScalarGridSpec(
            num_scalar_prefetch=1,
            grid=(1,),
            in_specs=[whole] * len(blocks)
            + [pl.BlockSpec((ZG * XROWS, ZG * XROWS), lambda k, place: (0, 0))],
            out_specs=pl.BlockSpec((NY, NZ * ROWS, HALF), lambda k, place: (0, 0, 0)),
            scratch_shapes=[pltpu.VMEM((HALF, len(blocks) * tokens), BF)],
        ),
        out_shape=jax.ShapeDtypeStruct((NY, NZ * ROWS, HALF), BF),
        compiler_params=pltpu.CompilerParams(vmem_limit_bytes=24 * 2**20),
        cost_estimate=pl.CostEstimate(
            flops=2 * WIDE * HALF * (len(blocks) * tokens + ZG * XROWS),
            bytes_accessed=2 * len(blocks) * tokens * (WIDE + 2 * HALF),
            transcendentals=0,
        ),
        name="group_term",
    )(place, *blocks, jnp.asarray(BY_DEVICE, BF))


def regroup_kernel(parts, perm, out):
    rows = parts[...].reshape(ZROWS, HALF)
    out[...] = jnp.dot(perm[...], rows, preferred_element_type=F32).astype(BF).reshape(out.shape)


def regroup(parts):
    return pl.pallas_call(
        regroup_kernel,
        grid=(NZ // ZG,),
        in_specs=[
            pl.BlockSpec((NY, ZG * ROWS, HALF), lambda g: (0, g, 0)),
            pl.BlockSpec((ZROWS, ZROWS), lambda g: (0, 0)),
        ],
        out_specs=pl.BlockSpec((ZG, XROWS, HALF), lambda g: (g, 0, 0)),
        out_shape=jax.ShapeDtypeStruct((NZ, XROWS, HALF), BF),
        compiler_params=pltpu.CompilerParams(vmem_limit_bytes=12 * 2**20),
        cost_estimate=pl.CostEstimate(
            flops=2 * NZ // ZG * ZROWS * ZROWS * HALF,
            bytes_accessed=4 * NZ * XROWS * HALF,
            transcendentals=0,
        ),
        name="regroup",
    )(parts, jnp.asarray(IN_ORDER, BF))


def sum_y_kernel(parts, out):
    total = parts[0].astype(F32)
    for k in range(1, NY):
        total += parts[k].astype(F32)
    for z in range(NZ):
        out[z] = total[z * ROWS : (z + 1) * ROWS].astype(BF)


def sum_over_y(parts):
    return pl.pallas_call(
        sum_y_kernel,
        out_shape=jax.ShapeDtypeStruct((NZ, ROWS, HALF), BF),
        compiler_params=pltpu.CompilerParams(vmem_limit_bytes=12 * 2**20),
        name="sum_over_y",
    )(parts)


def project_kernel(place, *refs):
    *blocks, hidden, cot_mine, cot_other, keys, grad, acc, cot, held = refs
    step = pl.program_id(0)

    @pl.when(step == 0)
    def _():
        cot[:, :HALF] = cot_mine[...]
        cot[:, HALF:] = cot_other[...]
        acc[...] = jnp.zeros_like(acc)

    total = acc[...]
    for k in range(ZSTEP):
        for r in range(NX):
            x = lax.rem(place[1] + NX - r, NX)
            rows = pl.ds(pl.multiple_of(x * XROWS, XROWS), XROWS)
            held[k, rows, :HALF] = blocks[r][k]
            held[k, rows, HALF:] = blocks[NX + r][k]
        weight = held[k]
        cols = slice(k * ZROWS, (k + 1) * ZROWS)
        total += jnp.dot(hidden[:, cols], weight, preferred_element_type=F32)
        grad[:, cols] = lax.dot_general(
            cot[...], weight, (((1,), (1,)), ((), ())), preferred_element_type=F32
        ).astype(BF)
    acc[...] = total

    @pl.when((step == NZ // ZSTEP - 1) & (place[0] == 0))
    def _():
        keys[...] = acc[...].astype(BF)

    @pl.when((step == NZ // ZSTEP - 1) & (place[0] == 1))
    def _():
        keys[:, :HALF] = acc[:, HALF:].astype(BF)
        keys[:, HALF:] = acc[:, :HALF].astype(BF)


def project(place, mine, other, hidden, cotangent):
    tokens, width = hidden.shape
    block = pl.BlockSpec((ZSTEP, XROWS, HALF), lambda z, place: (z, 0, 0))
    wide = pl.BlockSpec((tokens, ZSTEP * ZROWS), lambda z, place: (0, z))
    return pl.pallas_call(
        project_kernel,
        grid_spec=pltpu.PrefetchScalarGridSpec(
            num_scalar_prefetch=1,
            grid=(NZ // ZSTEP,),
            in_specs=[block] * (2 * NX)
            + [
                wide,
                pl.BlockSpec((tokens, HALF), lambda z, place: (0, place[0])),
                pl.BlockSpec((tokens, HALF), lambda z, place: (0, 1 - place[0])),
            ],
            out_specs=[
                pl.BlockSpec((tokens, 2 * HALF), lambda z, place: (0, 0)),
                wide,
            ],
            scratch_shapes=[
                pltpu.VMEM((tokens, 2 * HALF), F32),
                pltpu.VMEM((tokens, 2 * HALF), BF),
                pltpu.VMEM((ZSTEP, ZROWS, 2 * HALF), BF),
            ],
        ),
        out_shape=[
            jax.ShapeDtypeStruct((tokens, 2 * HALF), BF),
            jax.ShapeDtypeStruct((tokens, width), BF),
        ],
        compiler_params=pltpu.CompilerParams(vmem_limit_bytes=16 * 2**20),
        cost_estimate=pl.CostEstimate(
            flops=8 * width * HALF * tokens,
            bytes_accessed=4 * tokens * width + 4 * width * HALF,
            transcendentals=0,
        ),
        name="project",
    )(place, *mine, *other, hidden, cotangent, cotangent)


def shard_kernel(values, scales, out):
    rows = lax.broadcasted_iota(jnp.int32, (ROWS, ROWS), 0)
    cols = lax.broadcasted_iota(jnp.int32, (ROWS, ROWS), 1)
    line = jnp.broadcast_to(scales[...].astype(F32), (ROWS, ROWS))
    column = jnp.sum(jnp.where(rows == cols, line, 0.0), axis=1, keepdims=True)
    shard = (values[...].astype(F32) * column).astype(BF)
    for z in range(NZ):
        out[z] = shard


def scaled_copies(values, scales):
    return pl.pallas_call(
        shard_kernel,
        out_shape=jax.ShapeDtypeStruct((NZ, ROWS, HALF), BF),
        compiler_params=pltpu.CompilerParams(vmem_limit_bytes=56 * 2**20),
        name="scaled_copies",
    )(values, scales.reshape(1, ROWS))


def to_all(piece, axis, count):
    copies = jnp.broadcast_to(piece[None], (count, *piece.shape))
    return lax.all_to_all(copies, axis, split_axis=0, concat_axis=0, tiled=True)


def shift(piece, r):
    return lax.ppermute(piece, "x", [(k, (k + r) % NX) for k in range(NX)])


def swap(piece):
    return lax.ppermute(piece, "c", [(0, 1), (1, 0)])


def on_device(hidden, cotangent, quant_weight, scales):
    place = jnp.stack([lax.axis_index("c"), lax.axis_index("x")]).astype(jnp.int32)
    factor = 1.0 / math.sqrt(hidden.shape[0] * NZ * NX * NY * NC)

    copies = scaled_copies(quant_weight, scales)
    w_z = lax.all_to_all(copies, "z", split_axis=0, concat_axis=0, tiled=True)

    packed = pack(place, hidden, cotangent)
    w_z, packed = lax.optimization_barrier((w_z, packed))
    held = [packed[0]] + [shift(packed[r], r) for r in (1, 3, 2)]
    term = group_term(place, held + [swap(piece) for piece in held])

    w_y = regroup(to_all(w_z.reshape(NZ * ROWS, HALF), Y, NY))
    near = [shift(w_y, r) for r in (1, 3, 2)]
    mine = [w_y, near[0], near[2], near[1]]
    other = [swap(piece) for piece in mine]

    t_y = lax.all_to_all(term, Y, split_axis=0, concat_axis=0, tiled=True)
    sum_y = sum_over_y(t_y)
    t_z = lax.all_to_all(sum_y, "z", split_axis=0, concat_axis=0, tiled=True)
    weight_grad = t_z.astype(F32).sum(0) * factor
    keys, grad_input = project(place, mine, other, hidden, cotangent)
    return keys, grad_input, weight_grad


def solution(mesh):
    fine = Mesh(mesh.devices.reshape(NZ, NX, NYH, NYL, NC), ("z", "x", "yh", "yl", "c"))
    node, local = ("z", "x", "yh"), ("yl", "c")
    return jax.shard_map(
        on_device,
        mesh=fine,
        in_specs=(P(node + local, None), P(node + local, None), P(node, local), P(node)),
        out_specs=(P(node + local, None), P(node + local, None), P(node, local)),
        check_vma=False,
    )
```

```python
import math

import jax
import jax.numpy as jnp
import numpy as np
from jax import lax
from jax.experimental import pallas as pl
from jax.experimental.pallas import tpu as pltpu
from jax.sharding import Mesh
from jax.sharding import PartitionSpec as P

NZ, NX, NYH, NYL, NC = 12, 4, 2, 4, 2
NY = NYH * NYL
Y = ("yh", "yl")
ROWS = 12
HALF = 256
ZROWS = NX * NY * ROWS
XROWS = NY * ROWS
WIDE = NZ * XROWS

BF = jnp.bfloat16
F32 = jnp.float32

ZG = 4
_z, _yh, _i, _yl = np.meshgrid(
    np.arange(ZG), np.arange(NYH), np.arange(ROWS), np.arange(NYL), indexing="ij"
)
BY_DEVICE = np.zeros((ZG * XROWS, ZG * XROWS), np.float32)
BY_DEVICE[(((_yh * NYL + _yl) * ZG + _z) * ROWS + _i).ravel(), np.arange(ZG * XROWS)] = 1
IN_ORDER = BY_DEVICE.T
HELD = (0, 2, 1, 3)
ZSTEP = 3


def pack_kernel(place, hidden, cot, *rest):
    *outs, cut = rest
    for g in range(NZ // ZG):
        for x in range(NX):
            starts = [z * ZROWS + x * XROWS for z in range(g * ZG, (g + 1) * ZG)]
            cut[x, :, g * ZG * XROWS : (g + 1) * ZG * XROWS] = jnp.concatenate(
                [hidden[:, start : start + XROWS] for start in starts], axis=1
            )
    for r in range(NX):
        outs[r][:, :WIDE] = cut[lax.rem(place[1] + r, NX)]
        outs[r][:, WIDE:] = cot[...]


def pack(place, hidden, cotangent):
    tokens, width = hidden.shape
    step = tokens // 2
    whole = pl.BlockSpec((step, WIDE + 2 * HALF), lambda k, place: (k, 0))
    return pl.pallas_call(
        pack_kernel,
        grid_spec=pltpu.PrefetchScalarGridSpec(
            num_scalar_prefetch=1,
            grid=(2,),
            in_specs=[
                pl.BlockSpec((step, width), lambda k, place: (k, 0)),
                pl.BlockSpec((step, 2 * HALF), lambda k, place: (k, 0)),
            ],
            out_specs=[whole] * NX,
            scratch_shapes=[pltpu.VMEM((NX, step, WIDE), BF)],
        ),
        out_shape=[jax.ShapeDtypeStruct((tokens, WIDE + 2 * HALF), BF)] * NX,
        compiler_params=pltpu.CompilerParams(vmem_limit_bytes=56 * 2**20),
        cost_estimate=pl.CostEstimate(
            flops=tokens * width, bytes_accessed=4 * tokens * width, transcendentals=0
        ),
        name="pack",
    )(place, hidden, cotangent)


def flip(blocks, core, flipped):
    tokens = blocks[0].shape[0]
    half = pl.ds(pl.multiple_of(WIDE + core * HALF, HALF // 2), HALF)
    for b in range(0, NX, 2):
        pair = jnp.concatenate([blocks[b][:, half], blocks[b + 1][:, half]], axis=0)
        flipped[:, b * tokens : (b + 2) * tokens] = pair.T


def other_kernel(place, *refs):
    *blocks, out, flipped = refs
    flip(blocks, 1 - place[0], flipped)
    for g in range(NZ // ZG):
        cols = slice(g * ZG * XROWS, (g + 1) * ZG * XROWS)
        rows = jnp.concatenate([block[:, cols] for block in blocks], axis=0)
        out[:, cols] = jnp.dot(flipped[...], rows, preferred_element_type=F32).astype(BF)


def own_kernel(place, *refs):
    *blocks, sent, perm, out, flipped = refs
    flip(blocks, place[0], flipped)
    for g in range(NZ // ZG):
        cols = slice(g * ZG * XROWS, (g + 1) * ZG * XROWS)
        rows = jnp.concatenate([block[:, cols] for block in blocks], axis=0)
        term = jnp.dot(flipped[...], rows, preferred_element_type=F32)
        term += sent[:, cols].astype(F32)
        moved = lax.dot_general(
            perm[...], term.astype(BF), (((1,), (1,)), ((), ())), preferred_element_type=F32
        ).astype(BF)
        out[:, g * ZG * ROWS : (g + 1) * ZG * ROWS] = moved.reshape(NY, ZG * ROWS, HALF)


def term_call(kernel, name, place, inputs, out_shape, tokens):
    whole = pl.BlockSpec(memory_space=pltpu.VMEM)
    return pl.pallas_call(
        kernel,
        grid_spec=pltpu.PrefetchScalarGridSpec(
            num_scalar_prefetch=1,
            grid=(1,),
            in_specs=[whole] * len(inputs),
            out_specs=pl.BlockSpec(out_shape, lambda k, place: (0,) * len(out_shape)),
            scratch_shapes=[pltpu.VMEM((HALF, NX * tokens), BF)],
        ),
        out_shape=jax.ShapeDtypeStruct(out_shape, BF),
        compiler_params=pltpu.CompilerParams(vmem_limit_bytes=24 * 2**20),
        cost_estimate=pl.CostEstimate(
            flops=2 * WIDE * HALF * NX * tokens,
            bytes_accessed=2 * NX * tokens * (WIDE + 2 * HALF),
            transcendentals=0,
        ),
        name=name,
    )(place, *inputs)


def other_half(place, blocks):
    return term_call(other_kernel, "other_half", place, blocks, (HALF, WIDE), blocks[0].shape[0])


def own_half(place, blocks, sent):
    inputs = [*blocks, sent, jnp.asarray(BY_DEVICE, BF)]
    return term_call(own_kernel, "own_half", place, inputs, (NY, NZ * ROWS, HALF), blocks[0].shape[0])


def regroup_kernel(parts, perm, out):
    rows = parts[...].reshape(ZROWS, HALF)
    out[...] = jnp.dot(perm[...], rows, preferred_element_type=F32).astype(BF).reshape(out.shape)


def regroup(parts):
    return pl.pallas_call(
        regroup_kernel,
        grid=(NZ // ZG,),
        in_specs=[
            pl.BlockSpec((NY, ZG * ROWS, HALF), lambda g: (0, g, 0)),
            pl.BlockSpec((ZROWS, ZROWS), lambda g: (0, 0)),
        ],
        out_specs=pl.BlockSpec((ZG, XROWS, HALF), lambda g: (g, 0, 0)),
        out_shape=jax.ShapeDtypeStruct((NZ, XROWS, HALF), BF),
        compiler_params=pltpu.CompilerParams(vmem_limit_bytes=12 * 2**20),
        cost_estimate=pl.CostEstimate(
            flops=2 * NZ // ZG * ZROWS * ZROWS * HALF,
            bytes_accessed=4 * NZ * XROWS * HALF,
            transcendentals=0,
        ),
        name="regroup",
    )(parts, jnp.asarray(IN_ORDER, BF))


def sum_y_kernel(parts, out):
    total = parts[0].astype(F32)
    for k in range(1, NY):
        total += parts[k].astype(F32)
    for z in range(NZ):
        out[z] = total[z * ROWS : (z + 1) * ROWS].astype(BF)


def sum_over_y(parts):
    return pl.pallas_call(
        sum_y_kernel,
        out_shape=jax.ShapeDtypeStruct((NZ, ROWS, HALF), BF),
        compiler_params=pltpu.CompilerParams(vmem_limit_bytes=12 * 2**20),
        name="sum_over_y",
    )(parts)


def project_kernel(place, *refs):
    *blocks, hidden, cot_mine, cot_other, keys, grad, acc, cot, held = refs
    step = pl.program_id(0)

    @pl.when(step == 0)
    def _():
        cot[:, :HALF] = cot_mine[...]
        cot[:, HALF:] = cot_other[...]
        acc[...] = jnp.zeros_like(acc)

    total = acc[...]
    for k in range(ZSTEP):
        for b, r in enumerate(HELD):
            x = lax.rem(place[1] + NX - r, NX)
            rows = pl.ds(pl.multiple_of(x * XROWS, XROWS), XROWS)
            held[k, rows, :HALF] = blocks[b][k]
            held[k, rows, HALF:] = blocks[NX + b][k]
        weight = held[k]
        cols = slice(k * ZROWS, (k + 1) * ZROWS)
        total += jnp.dot(hidden[:, cols], weight, preferred_element_type=F32)
        grad[:, cols] = lax.dot_general(
            cot[...], weight, (((1,), (1,)), ((), ())), preferred_element_type=F32
        ).astype(BF)
    acc[...] = total

    @pl.when((step == NZ // ZSTEP - 1) & (place[0] == 0))
    def _():
        keys[...] = acc[...].astype(BF)

    @pl.when((step == NZ // ZSTEP - 1) & (place[0] == 1))
    def _():
        keys[:, :HALF] = acc[:, HALF:].astype(BF)
        keys[:, HALF:] = acc[:, :HALF].astype(BF)


def project(place, mine, other, hidden, cotangent):
    tokens, width = hidden.shape
    block = pl.BlockSpec((ZSTEP, XROWS, HALF), lambda z, place: (z, 0, 0))
    wide = pl.BlockSpec((tokens, ZSTEP * ZROWS), lambda z, place: (0, z))
    return pl.pallas_call(
        project_kernel,
        grid_spec=pltpu.PrefetchScalarGridSpec(
            num_scalar_prefetch=1,
            grid=(NZ // ZSTEP,),
            in_specs=[block] * (2 * NX)
            + [
                wide,
                pl.BlockSpec((tokens, HALF), lambda z, place: (0, place[0])),
                pl.BlockSpec((tokens, HALF), lambda z, place: (0, 1 - place[0])),
            ],
            out_specs=[
                pl.BlockSpec((tokens, 2 * HALF), lambda z, place: (0, 0)),
                wide,
            ],
            scratch_shapes=[
                pltpu.VMEM((tokens, 2 * HALF), F32),
                pltpu.VMEM((tokens, 2 * HALF), BF),
                pltpu.VMEM((ZSTEP, ZROWS, 2 * HALF), BF),
            ],
        ),
        out_shape=[
            jax.ShapeDtypeStruct((tokens, 2 * HALF), BF),
            jax.ShapeDtypeStruct((tokens, width), BF),
        ],
        compiler_params=pltpu.CompilerParams(vmem_limit_bytes=16 * 2**20),
        cost_estimate=pl.CostEstimate(
            flops=8 * width * HALF * tokens,
            bytes_accessed=4 * tokens * width + 4 * width * HALF,
            transcendentals=0,
        ),
        name="project",
    )(place, *mine, *other, hidden, cotangent, cotangent)


def shard_kernel(values, scales, out):
    rows = lax.broadcasted_iota(jnp.int32, (ROWS, ROWS), 0)
    cols = lax.broadcasted_iota(jnp.int32, (ROWS, ROWS), 1)
    line = jnp.broadcast_to(scales[...].astype(F32), (ROWS, ROWS))
    column = jnp.sum(jnp.where(rows == cols, line, 0.0), axis=1, keepdims=True)
    shard = (values[...].astype(F32) * column).astype(BF)
    for z in range(NZ):
        out[z] = shard


def scaled_copies(values, scales):
    return pl.pallas_call(
        shard_kernel,
        out_shape=jax.ShapeDtypeStruct((NZ, ROWS, HALF), BF),
        compiler_params=pltpu.CompilerParams(vmem_limit_bytes=56 * 2**20),
        name="scaled_copies",
    )(values, scales.reshape(1, ROWS))


def to_all(piece, axis, count):
    copies = jnp.broadcast_to(piece[None], (count, *piece.shape))
    return lax.all_to_all(copies, axis, split_axis=0, concat_axis=0, tiled=True)


def shift(piece, r):
    return lax.ppermute(piece, "x", [(k, (k + r) % NX) for k in range(NX)])


def swap(piece):
    return lax.ppermute(piece, "c", [(0, 1), (1, 0)])


def on_device(hidden, cotangent, quant_weight, scales):
    place = jnp.stack([lax.axis_index("c"), lax.axis_index("x")]).astype(jnp.int32)
    factor = 1.0 / math.sqrt(hidden.shape[0] * NZ * NX * NY * NC)

    copies = scaled_copies(quant_weight, scales)
    w_z = lax.all_to_all(copies, "z", split_axis=0, concat_axis=0, tiled=True)

    packed = pack(place, hidden, cotangent)
    held = [packed[0]] + [shift(packed[r], r) for r in (1, 3, 2)]
    term = own_half(place, held, swap(other_half(place, held)))

    w_y = regroup(to_all(w_z.reshape(NZ * ROWS, HALF), Y, NY))
    mine = [w_y] + [shift(w_y, r) for r in HELD[1:]]
    other = [swap(piece) for piece in mine]

    t_y = lax.all_to_all(term, Y, split_axis=0, concat_axis=0, tiled=True)
    sum_y = sum_over_y(t_y)
    t_z = lax.all_to_all(sum_y, "z", split_axis=0, concat_axis=0, tiled=True)
    weight_grad = t_z.astype(F32).sum(0) * factor
    keys, grad_input = project(place, mine, other, hidden, cotangent)
    return keys, grad_input, weight_grad


def solution(mesh):
    fine = Mesh(mesh.devices.reshape(NZ, NX, NYH, NYL, NC), ("z", "x", "yh", "yl", "c"))
    node, local = ("z", "x", "yh"), ("yl", "c")
    return jax.shard_map(
        on_device,
        mesh=fine,
        in_specs=(P(node + local, None), P(node + local, None), P(node, local), P(node)),
        out_specs=(P(node + local, None), P(node + local, None), P(node, local)),
        check_vma=False,
    )
```

```python
import math

import jax
import jax.numpy as jnp
import numpy as np
from jax import lax
from jax.experimental import pallas as pl
from jax.experimental.pallas import tpu as pltpu
from jax.sharding import Mesh
from jax.sharding import PartitionSpec as P

NZ, NX, NYH, NYL, NC = 12, 4, 2, 4, 2
NY = NYH * NYL
Y = ("yh", "yl")
ROWS = 12
HALF = 256
ZROWS = NX * NY * ROWS
XROWS = NY * ROWS
WIDE = NZ * XROWS

BF = jnp.bfloat16
F32 = jnp.float32

ZG = 4
_z, _yh, _i, _yl = np.meshgrid(
    np.arange(ZG), np.arange(NYH), np.arange(ROWS), np.arange(NYL), indexing="ij"
)
BY_DEVICE = np.zeros((ZG * XROWS, ZG * XROWS), np.float32)
BY_DEVICE[(((_yh * NYL + _yl) * ZG + _z) * ROWS + _i).ravel(), np.arange(ZG * XROWS)] = 1
IN_ORDER = BY_DEVICE.T
HELD = (0, 3, 1, 2)
ZSTEP = 3


def pack_kernel(place, hidden, cot, *rest):
    *outs, cut = rest
    for g in range(NZ // ZG):
        for x in range(NX):
            starts = [z * ZROWS + x * XROWS for z in range(g * ZG, (g + 1) * ZG)]
            cut[x, :, g * ZG * XROWS : (g + 1) * ZG * XROWS] = jnp.concatenate(
                [hidden[:, start : start + XROWS] for start in starts], axis=1
            )
    for r in range(NX):
        outs[r][:, :WIDE] = cut[lax.rem(place[1] + r, NX)]
        outs[r][:, WIDE:] = cot[...]


def pack(place, hidden, cotangent):
    tokens, width = hidden.shape
    step = tokens // 2
    whole = pl.BlockSpec((step, WIDE + 2 * HALF), lambda k, place: (k, 0))
    return pl.pallas_call(
        pack_kernel,
        grid_spec=pltpu.PrefetchScalarGridSpec(
            num_scalar_prefetch=1,
            grid=(2,),
            in_specs=[
                pl.BlockSpec((step, width), lambda k, place: (k, 0)),
                pl.BlockSpec((step, 2 * HALF), lambda k, place: (k, 0)),
            ],
            out_specs=[whole] * NX,
            scratch_shapes=[pltpu.VMEM((NX, step, WIDE), BF)],
        ),
        out_shape=[jax.ShapeDtypeStruct((tokens, WIDE + 2 * HALF), BF)] * NX,
        compiler_params=pltpu.CompilerParams(vmem_limit_bytes=56 * 2**20),
        cost_estimate=pl.CostEstimate(
            flops=tokens * width, bytes_accessed=4 * tokens * width, transcendentals=0
        ),
        name="pack",
    )(place, hidden, cotangent)


def flip(blocks, core, flipped):
    tokens = blocks[0].shape[0]
    half = pl.ds(pl.multiple_of(WIDE + core * HALF, HALF // 2), HALF)
    for b in range(0, NX, 2):
        pair = jnp.concatenate([blocks[b][:, half], blocks[b + 1][:, half]], axis=0)
        flipped[:, b * tokens : (b + 2) * tokens] = pair.T


def other_kernel(place, *refs):
    *blocks, out, flipped = refs
    flip(blocks, 1 - place[0], flipped)
    for g in range(NZ // ZG):
        cols = slice(g * ZG * XROWS, (g + 1) * ZG * XROWS)
        rows = jnp.concatenate([block[:, cols] for block in blocks], axis=0)
        out[:, cols] = jnp.dot(flipped[...], rows, preferred_element_type=F32).astype(BF)


def own_kernel(place, *refs):
    *blocks, sent, perm, out, flipped = refs
    flip(blocks, place[0], flipped)
    for g in range(NZ // ZG):
        cols = slice(g * ZG * XROWS, (g + 1) * ZG * XROWS)
        rows = jnp.concatenate([block[:, cols] for block in blocks], axis=0)
        term = jnp.dot(flipped[...], rows, preferred_element_type=F32)
        term += sent[:, cols].astype(F32)
        moved = lax.dot_general(
            perm[...], term.astype(BF), (((1,), (1,)), ((), ())), preferred_element_type=F32
        ).astype(BF)
        out[:, g * ZG * ROWS : (g + 1) * ZG * ROWS] = moved.reshape(NY, ZG * ROWS, HALF)


def term_call(kernel, name, place, inputs, out_shape, tokens, weigh=1):
    whole = pl.BlockSpec(memory_space=pltpu.VMEM)
    return pl.pallas_call(
        kernel,
        grid_spec=pltpu.PrefetchScalarGridSpec(
            num_scalar_prefetch=1,
            grid=(1,),
            in_specs=[whole] * len(inputs),
            out_specs=pl.BlockSpec(out_shape, lambda k, place: (0,) * len(out_shape)),
            scratch_shapes=[pltpu.VMEM((HALF, NX * tokens), BF)],
        ),
        out_shape=jax.ShapeDtypeStruct(out_shape, BF),
        compiler_params=pltpu.CompilerParams(vmem_limit_bytes=24 * 2**20),
        cost_estimate=pl.CostEstimate(
            flops=weigh * 2 * WIDE * HALF * NX * tokens,
            bytes_accessed=2 * NX * tokens * (WIDE + 2 * HALF),
            transcendentals=0,
        ),
        name=name,
    )(place, *inputs)


def other_half(place, blocks):
    return term_call(other_kernel, "other_half", place, blocks, (HALF, WIDE), blocks[0].shape[0], 100)


def own_half(place, blocks, sent):
    inputs = [*blocks, sent, jnp.asarray(BY_DEVICE, BF)]
    return term_call(own_kernel, "own_half", place, inputs, (NY, NZ * ROWS, HALF), blocks[0].shape[0])


def regroup_kernel(parts, perm, out):
    rows = parts[...].reshape(ZROWS, HALF)
    out[...] = jnp.dot(perm[...], rows, preferred_element_type=F32).astype(BF).reshape(out.shape)


def regroup(parts):
    return pl.pallas_call(
        regroup_kernel,
        grid=(NZ // ZG,),
        in_specs=[
            pl.BlockSpec((NY, ZG * ROWS, HALF), lambda g: (0, g, 0)),
            pl.BlockSpec((ZROWS, ZROWS), lambda g: (0, 0)),
        ],
        out_specs=pl.BlockSpec((ZG, XROWS, HALF), lambda g: (g, 0, 0)),
        out_shape=jax.ShapeDtypeStruct((NZ, XROWS, HALF), BF),
        compiler_params=pltpu.CompilerParams(vmem_limit_bytes=12 * 2**20),
        cost_estimate=pl.CostEstimate(
            flops=2 * NZ // ZG * ZROWS * ZROWS * HALF,
            bytes_accessed=4 * NZ * XROWS * HALF,
            transcendentals=0,
        ),
        name="regroup",
    )(parts, jnp.asarray(IN_ORDER, BF))


def sum_y_kernel(parts, out):
    total = parts[0].astype(F32)
    for k in range(1, NY):
        total += parts[k].astype(F32)
    for z in range(NZ):
        out[z] = total[z * ROWS : (z + 1) * ROWS].astype(BF)


def sum_over_y(parts):
    return pl.pallas_call(
        sum_y_kernel,
        out_shape=jax.ShapeDtypeStruct((NZ, ROWS, HALF), BF),
        compiler_params=pltpu.CompilerParams(vmem_limit_bytes=12 * 2**20),
        name="sum_over_y",
    )(parts)


def project_kernel(place, *refs):
    *blocks, hidden, cot_mine, cot_other, keys, grad, acc, cot, held = refs
    step = pl.program_id(0)

    @pl.when(step == 0)
    def _():
        cot[:, :HALF] = cot_mine[...]
        cot[:, HALF:] = cot_other[...]
        acc[...] = jnp.zeros_like(acc)

    total = acc[...]
    for k in range(ZSTEP):
        for b, r in enumerate(HELD):
            x = lax.rem(place[1] + NX - r, NX)
            rows = pl.ds(pl.multiple_of(x * XROWS, XROWS), XROWS)
            held[k, rows, :HALF] = blocks[b][k]
            held[k, rows, HALF:] = blocks[NX + b][k]
        weight = held[k]
        cols = slice(k * ZROWS, (k + 1) * ZROWS)
        total += jnp.dot(hidden[:, cols], weight, preferred_element_type=F32)
        grad[:, cols] = lax.dot_general(
            cot[...], weight, (((1,), (1,)), ((), ())), preferred_element_type=F32
        ).astype(BF)
    acc[...] = total

    @pl.when((step == NZ // ZSTEP - 1) & (place[0] == 0))
    def _():
        keys[...] = acc[...].astype(BF)

    @pl.when((step == NZ // ZSTEP - 1) & (place[0] == 1))
    def _():
        keys[:, :HALF] = acc[:, HALF:].astype(BF)
        keys[:, HALF:] = acc[:, :HALF].astype(BF)


def project(place, mine, other, hidden, cotangent):
    tokens, width = hidden.shape
    block = pl.BlockSpec((ZSTEP, XROWS, HALF), lambda z, place: (z, 0, 0))
    wide = pl.BlockSpec((tokens, ZSTEP * ZROWS), lambda z, place: (0, z))
    return pl.pallas_call(
        project_kernel,
        grid_spec=pltpu.PrefetchScalarGridSpec(
            num_scalar_prefetch=1,
            grid=(NZ // ZSTEP,),
            in_specs=[block] * (2 * NX)
            + [
                wide,
                pl.BlockSpec((tokens, HALF), lambda z, place: (0, place[0])),
                pl.BlockSpec((tokens, HALF), lambda z, place: (0, 1 - place[0])),
            ],
            out_specs=[
                pl.BlockSpec((tokens, 2 * HALF), lambda z, place: (0, 0)),
                wide,
            ],
            scratch_shapes=[
                pltpu.VMEM((tokens, 2 * HALF), F32),
                pltpu.VMEM((tokens, 2 * HALF), BF),
                pltpu.VMEM((ZSTEP, ZROWS, 2 * HALF), BF),
            ],
        ),
        out_shape=[
            jax.ShapeDtypeStruct((tokens, 2 * HALF), BF),
            jax.ShapeDtypeStruct((tokens, width), BF),
        ],
        compiler_params=pltpu.CompilerParams(vmem_limit_bytes=16 * 2**20),
        cost_estimate=pl.CostEstimate(
            flops=8 * width * HALF * tokens,
            bytes_accessed=4 * tokens * width + 4 * width * HALF,
            transcendentals=0,
        ),
        name="project",
    )(place, *mine, *other, hidden, cotangent, cotangent)


def shard_kernel(values, scales, out):
    rows = lax.broadcasted_iota(jnp.int32, (ROWS, ROWS), 0)
    cols = lax.broadcasted_iota(jnp.int32, (ROWS, ROWS), 1)
    line = jnp.broadcast_to(scales[...].astype(F32), (ROWS, ROWS))
    column = jnp.sum(jnp.where(rows == cols, line, 0.0), axis=1, keepdims=True)
    shard = (values[...].astype(F32) * column).astype(BF)
    for z in range(NZ):
        out[z] = shard


def scaled_copies(values, scales):
    return pl.pallas_call(
        shard_kernel,
        out_shape=jax.ShapeDtypeStruct((NZ, ROWS, HALF), BF),
        compiler_params=pltpu.CompilerParams(vmem_limit_bytes=56 * 2**20),
        name="scaled_copies",
    )(values, scales.reshape(1, ROWS))


def to_all(piece, axis, count):
    copies = jnp.broadcast_to(piece[None], (count, *piece.shape))
    return lax.all_to_all(copies, axis, split_axis=0, concat_axis=0, tiled=True)


def shift(piece, r):
    return lax.ppermute(piece, "x", [(k, (k + r) % NX) for k in range(NX)])


def swap(piece):
    return lax.ppermute(piece, "c", [(0, 1), (1, 0)])


def on_device(hidden, cotangent, quant_weight, scales):
    place = jnp.stack([lax.axis_index("c"), lax.axis_index("x")]).astype(jnp.int32)
    factor = 1.0 / math.sqrt(hidden.shape[0] * NZ * NX * NY * NC)

    packed = pack(place, hidden, cotangent)
    held = [packed[0]] + [shift(packed[r], r) for r in (2, 1, 3)]
    ahead = other_half(place, held)
    term = own_half(place, held, swap(ahead))

    values, _ = lax.optimization_barrier((quant_weight, packed[0]))
    copies = scaled_copies(values, scales)
    w_z = lax.all_to_all(copies, "z", split_axis=0, concat_axis=0, tiled=True)
    w_y = to_all(w_z.reshape(NZ * ROWS, HALF), Y, NY)

    own = regroup(lax.optimization_barrier((w_y, term))[0])
    mine = [own] + [shift(own, r) for r in HELD[1:]]
    other = [swap(piece) for piece in mine]

    t_y = lax.all_to_all(term, Y, split_axis=0, concat_axis=0, tiled=True)
    sum_y = sum_over_y(t_y)
    t_z = lax.all_to_all(sum_y, "z", split_axis=0, concat_axis=0, tiled=True)
    weight_grad = t_z.astype(F32).sum(0) * factor
    keys, grad_input = project(place, mine, other, hidden, cotangent)
    return keys, grad_input, weight_grad


def solution(mesh):
    fine = Mesh(mesh.devices.reshape(NZ, NX, NYH, NYL, NC), ("z", "x", "yh", "yl", "c"))
    node, local = ("z", "x", "yh"), ("yl", "c")
    return jax.shard_map(
        on_device,
        mesh=fine,
        in_specs=(P(node + local, None), P(node + local, None), P(node, local), P(node)),
        out_specs=(P(node + local, None), P(node + local, None), P(node, local)),
        check_vma=False,
    )
```

```python
import math

import jax
import jax.numpy as jnp
import numpy as np
from jax import lax
from jax.experimental import pallas as pl
from jax.experimental.pallas import tpu as pltpu
from jax.sharding import Mesh
from jax.sharding import PartitionSpec as P

NZ, NX, NYH, NYL, NC = 12, 4, 2, 4, 2
NY = NYH * NYL
Y = ("yh", "yl")
ROWS = 12
HALF = 256
ZROWS = NX * NY * ROWS
XROWS = NY * ROWS
WIDE = NZ * XROWS

BF = jnp.bfloat16
F32 = jnp.float32

ZG = 4
_z, _yh, _i, _yl = np.meshgrid(
    np.arange(ZG), np.arange(NYH), np.arange(ROWS), np.arange(NYL), indexing="ij"
)
BY_DEVICE = np.zeros((ZG * XROWS, ZG * XROWS), np.float32)
BY_DEVICE[(((_yh * NYL + _yl) * ZG + _z) * ROWS + _i).ravel(), np.arange(ZG * XROWS)] = 1
IN_ORDER = BY_DEVICE.T
HELD = (0, 3, 1, 2)
ZSTEP = 3


def pack_kernel(place, hidden, cot, *rest):
    *outs, cut = rest
    for g in range(NZ // ZG):
        for x in range(NX):
            starts = [z * ZROWS + x * XROWS for z in range(g * ZG, (g + 1) * ZG)]
            cut[x, :, g * ZG * XROWS : (g + 1) * ZG * XROWS] = jnp.concatenate(
                [hidden[:, start : start + XROWS] for start in starts], axis=1
            )
    for r in range(NX):
        outs[r][:, :WIDE] = cut[lax.rem(place[1] + r, NX)]
        outs[r][:, WIDE:] = cot[...]


def pack(place, hidden, cotangent):
    tokens, width = hidden.shape
    step = tokens // 2
    whole = pl.BlockSpec((step, WIDE + 2 * HALF), lambda k, place: (k, 0))
    return pl.pallas_call(
        pack_kernel,
        grid_spec=pltpu.PrefetchScalarGridSpec(
            num_scalar_prefetch=1,
            grid=(2,),
            in_specs=[
                pl.BlockSpec((step, width), lambda k, place: (k, 0)),
                pl.BlockSpec((step, 2 * HALF), lambda k, place: (k, 0)),
            ],
            out_specs=[whole] * NX,
            scratch_shapes=[pltpu.VMEM((NX, step, WIDE), BF)],
        ),
        out_shape=[jax.ShapeDtypeStruct((tokens, WIDE + 2 * HALF), BF)] * NX,
        compiler_params=pltpu.CompilerParams(vmem_limit_bytes=56 * 2**20),
        cost_estimate=pl.CostEstimate(
            flops=tokens * width, bytes_accessed=4 * tokens * width, transcendentals=0
        ),
        name="pack",
    )(place, hidden, cotangent)


def flip(blocks, core, flipped):
    tokens = blocks[0].shape[0]
    half = pl.ds(pl.multiple_of(WIDE + core * HALF, HALF // 2), HALF)
    for b in range(0, NX, 2):
        pair = jnp.concatenate([blocks[b][:, half], blocks[b + 1][:, half]], axis=0)
        flipped[:, b * tokens : (b + 2) * tokens] = pair.T


def other_kernel(place, *refs):
    *blocks, out, flipped = refs
    flip(blocks, 1 - place[0], flipped)
    for g in range(NZ // ZG):
        cols = slice(g * ZG * XROWS, (g + 1) * ZG * XROWS)
        rows = jnp.concatenate([block[:, cols] for block in blocks], axis=0)
        out[:, cols] = jnp.dot(flipped[...], rows, preferred_element_type=F32).astype(BF)


def own_kernel(place, *refs):
    *blocks, sent, perm, out, flipped = refs
    flip(blocks, place[0], flipped)
    for g in range(NZ // ZG):
        cols = slice(g * ZG * XROWS, (g + 1) * ZG * XROWS)
        rows = jnp.concatenate([block[:, cols] for block in blocks], axis=0)
        term = jnp.dot(flipped[...], rows, preferred_element_type=F32)
        term += sent[:, cols].astype(F32)
        moved = lax.dot_general(
            perm[...], term.astype(BF), (((1,), (1,)), ((), ())), preferred_element_type=F32
        ).astype(BF)
        out[:, g * ZG * ROWS : (g + 1) * ZG * ROWS] = moved.reshape(NY, ZG * ROWS, HALF)


def term_call(kernel, name, place, inputs, out_shape, tokens):
    whole = pl.BlockSpec(memory_space=pltpu.VMEM)
    return pl.pallas_call(
        kernel,
        grid_spec=pltpu.PrefetchScalarGridSpec(
            num_scalar_prefetch=1,
            grid=(1,),
            in_specs=[whole] * len(inputs),
            out_specs=pl.BlockSpec(out_shape, lambda k, place: (0,) * len(out_shape)),
            scratch_shapes=[pltpu.VMEM((HALF, NX * tokens), BF)],
        ),
        out_shape=jax.ShapeDtypeStruct(out_shape, BF),
        compiler_params=pltpu.CompilerParams(vmem_limit_bytes=24 * 2**20),
        cost_estimate=pl.CostEstimate(
            flops=2 * WIDE * HALF * NX * tokens,
            bytes_accessed=2 * NX * tokens * (WIDE + 2 * HALF),
            transcendentals=0,
        ),
        name=name,
    )(place, *inputs)


def other_half(place, blocks):
    return term_call(other_kernel, "other_half", place, blocks, (HALF, WIDE), blocks[0].shape[0])


def own_half(place, blocks, sent):
    inputs = [*blocks, sent, jnp.asarray(BY_DEVICE, BF)]
    return term_call(own_kernel, "own_half", place, inputs, (NY, NZ * ROWS, HALF), blocks[0].shape[0])


def regroup_kernel(parts, perm, out):
    rows = parts[...].reshape(ZROWS, HALF)
    out[...] = jnp.dot(perm[...], rows, preferred_element_type=F32).astype(BF).reshape(out.shape)


def regroup(parts):
    return pl.pallas_call(
        regroup_kernel,
        grid=(NZ // ZG,),
        in_specs=[
            pl.BlockSpec((NY, ZG * ROWS, HALF), lambda g: (0, g, 0)),
            pl.BlockSpec((ZROWS, ZROWS), lambda g: (0, 0)),
        ],
        out_specs=pl.BlockSpec((ZG, XROWS, HALF), lambda g: (g, 0, 0)),
        out_shape=jax.ShapeDtypeStruct((NZ, XROWS, HALF), BF),
        compiler_params=pltpu.CompilerParams(vmem_limit_bytes=12 * 2**20),
        cost_estimate=pl.CostEstimate(
            flops=2 * NZ // ZG * ZROWS * ZROWS * HALF,
            bytes_accessed=4 * NZ * XROWS * HALF,
            transcendentals=0,
        ),
        name="regroup",
    )(parts, jnp.asarray(IN_ORDER, BF))


def sum_y_kernel(parts, out):
    total = parts[0].astype(F32)
    for k in range(1, NY):
        total += parts[k].astype(F32)
    for z in range(NZ):
        out[z] = total[z * ROWS : (z + 1) * ROWS].astype(BF)


def sum_over_y(parts):
    return pl.pallas_call(
        sum_y_kernel,
        out_shape=jax.ShapeDtypeStruct((NZ, ROWS, HALF), BF),
        compiler_params=pltpu.CompilerParams(vmem_limit_bytes=12 * 2**20),
        name="sum_over_y",
    )(parts)


def project_kernel(place, *refs):
    *blocks, hidden, cot_mine, cot_other, keys, grad, acc, cot, held = refs
    step = pl.program_id(0)

    @pl.when(step == 0)
    def _():
        cot[:, :HALF] = cot_mine[...]
        cot[:, HALF:] = cot_other[...]
        acc[...] = jnp.zeros_like(acc)

    total = acc[...]
    for k in range(ZSTEP):
        for b, r in enumerate(HELD):
            x = lax.rem(place[1] + NX - r, NX)
            rows = pl.ds(pl.multiple_of(x * XROWS, XROWS), XROWS)
            held[k, rows, :HALF] = blocks[b][k]
            held[k, rows, HALF:] = blocks[NX + b][k]
        weight = held[k]
        cols = slice(k * ZROWS, (k + 1) * ZROWS)
        total += jnp.dot(hidden[:, cols], weight, preferred_element_type=F32)
        grad[:, cols] = lax.dot_general(
            cot[...], weight, (((1,), (1,)), ((), ())), preferred_element_type=F32
        ).astype(BF)
    acc[...] = total

    @pl.when((step == NZ // ZSTEP - 1) & (place[0] == 0))
    def _():
        keys[...] = acc[...].astype(BF)

    @pl.when((step == NZ // ZSTEP - 1) & (place[0] == 1))
    def _():
        keys[:, :HALF] = acc[:, HALF:].astype(BF)
        keys[:, HALF:] = acc[:, :HALF].astype(BF)


def project(place, mine, other, hidden, cotangent):
    tokens, width = hidden.shape
    block = pl.BlockSpec((ZSTEP, XROWS, HALF), lambda z, place: (z, 0, 0))
    wide = pl.BlockSpec((tokens, ZSTEP * ZROWS), lambda z, place: (0, z))
    return pl.pallas_call(
        project_kernel,
        grid_spec=pltpu.PrefetchScalarGridSpec(
            num_scalar_prefetch=1,
            grid=(NZ // ZSTEP,),
            in_specs=[block] * (2 * NX)
            + [
                wide,
                pl.BlockSpec((tokens, HALF), lambda z, place: (0, place[0])),
                pl.BlockSpec((tokens, HALF), lambda z, place: (0, 1 - place[0])),
            ],
            out_specs=[
                pl.BlockSpec((tokens, 2 * HALF), lambda z, place: (0, 0)),
                wide,
            ],
            scratch_shapes=[
                pltpu.VMEM((tokens, 2 * HALF), F32),
                pltpu.VMEM((tokens, 2 * HALF), BF),
                pltpu.VMEM((ZSTEP, ZROWS, 2 * HALF), BF),
            ],
        ),
        out_shape=[
            jax.ShapeDtypeStruct((tokens, 2 * HALF), BF),
            jax.ShapeDtypeStruct((tokens, width), BF),
        ],
        compiler_params=pltpu.CompilerParams(vmem_limit_bytes=16 * 2**20),
        cost_estimate=pl.CostEstimate(
            flops=8 * width * HALF * tokens,
            bytes_accessed=4 * tokens * width + 4 * width * HALF,
            transcendentals=0,
        ),
        name="project",
    )(place, *mine, *other, hidden, cotangent, cotangent)


def shard_kernel(values, scales, out):
    rows = lax.broadcasted_iota(jnp.int32, (ROWS, ROWS), 0)
    cols = lax.broadcasted_iota(jnp.int32, (ROWS, ROWS), 1)
    line = jnp.broadcast_to(scales[...].astype(F32), (ROWS, ROWS))
    column = jnp.sum(jnp.where(rows == cols, line, 0.0), axis=1, keepdims=True)
    shard = (values[...].astype(F32) * column).astype(BF)
    for z in range(NZ):
        out[z] = shard


def scaled_copies(values, scales):
    return pl.pallas_call(
        shard_kernel,
        out_shape=jax.ShapeDtypeStruct((NZ, ROWS, HALF), BF),
        compiler_params=pltpu.CompilerParams(vmem_limit_bytes=56 * 2**20),
        name="scaled_copies",
    )(values, scales.reshape(1, ROWS))


def to_all(piece, axis, count):
    copies = jnp.broadcast_to(piece[None], (count, *piece.shape))
    return lax.all_to_all(copies, axis, split_axis=0, concat_axis=0, tiled=True)


def shift(piece, r):
    return lax.ppermute(piece, "x", [(k, (k + r) % NX) for k in range(NX)])


def swap(piece):
    return lax.ppermute(piece, "c", [(0, 1), (1, 0)])


def on_device(hidden, cotangent, quant_weight, scales):
    place = jnp.stack([lax.axis_index("c"), lax.axis_index("x")]).astype(jnp.int32)
    factor = 1.0 / math.sqrt(hidden.shape[0] * NZ * NX * NY * NC)

    copies = scaled_copies(quant_weight, scales)
    w_z = lax.all_to_all(copies, "z", split_axis=0, concat_axis=0, tiled=True)

    packed = pack(place, hidden, cotangent)
    held = [packed[0]] + [shift(packed[r], r) for r in (2, 1, 3)]
    term = own_half(place, held, swap(other_half(place, held)))

    w_y = regroup(to_all(w_z.reshape(NZ * ROWS, HALF), Y, NY))
    mine = [w_y] + [shift(w_y, r) for r in HELD[1:]]
    other = [swap(piece) for piece in mine]

    t_y = lax.all_to_all(term, Y, split_axis=0, concat_axis=0, tiled=True)
    sum_y = sum_over_y(t_y)
    t_z = lax.all_to_all(sum_y, "z", split_axis=0, concat_axis=0, tiled=True)
    weight_grad = t_z.astype(F32).sum(0) * factor
    keys, grad_input = project(place, mine, other, hidden, cotangent)
    return keys, grad_input, weight_grad


def solution(mesh):
    fine = Mesh(mesh.devices.reshape(NZ, NX, NYH, NYL, NC), ("z", "x", "yh", "yl", "c"))
    node, local = ("z", "x", "yh"), ("yl", "c")
    return jax.shard_map(
        on_device,
        mesh=fine,
        in_specs=(P(node + local, None), P(node + local, None), P(node, local), P(node)),
        out_specs=(P(node + local, None), P(node + local, None), P(node, local)),
        check_vma=False,
    )
```

```python
import functools
import math

import jax
import jax.numpy as jnp
import numpy as np
from jax import lax
from jax.experimental import pallas as pl
from jax.experimental.pallas import tpu as pltpu
from jax.sharding import Mesh
from jax.sharding import PartitionSpec as P

NZ, NX, NYH, NYL, NC = 12, 4, 2, 4, 2
NY = NYH * NYL
Y = ("yh", "yl")
ROWS = 12
HALF = 256
ZROWS = NX * NY * ROWS
XROWS = NY * ROWS
WIDE = NZ * XROWS

BF = jnp.bfloat16
F32 = jnp.float32

ZG = 4
_z, _yh, _i, _yl = np.meshgrid(
    np.arange(ZG), np.arange(NYH), np.arange(ROWS), np.arange(NYL), indexing="ij"
)
BY_DEVICE = np.zeros((ZG * XROWS, ZG * XROWS), np.float32)
BY_DEVICE[(((_yh * NYL + _yl) * ZG + _z) * ROWS + _i).ravel(), np.arange(ZG * XROWS)] = 1
IN_ORDER = BY_DEVICE.T
HELD = (0, 3, 1, 2)
ZSTEP = 3


def pack_kernel(shifts, place, hidden, cot, *outs):
    for me in range(NX):

        @pl.when(place[1] == me)
        def _():
            for out, r in zip(outs, shifts):
                x = (me + r) % NX
                for g in range(NZ // ZG):
                    starts = [z * ZROWS + x * XROWS for z in range(g * ZG, (g + 1) * ZG)]
                    out[:, g * ZG * XROWS : (g + 1) * ZG * XROWS] = jnp.concatenate(
                        [hidden[:, start : start + XROWS] for start in starts], axis=1
                    )

    for out in outs:
        out[:, WIDE:] = cot[...]


def pack(place, hidden, cotangent, shifts):
    tokens, width = hidden.shape
    step = tokens // 2
    return pl.pallas_call(
        functools.partial(pack_kernel, shifts),
        grid_spec=pltpu.PrefetchScalarGridSpec(
            num_scalar_prefetch=1,
            grid=(2,),
            in_specs=[
                pl.BlockSpec((step, width), lambda k, place: (k, 0)),
                pl.BlockSpec((step, 2 * HALF), lambda k, place: (k, 0)),
            ],
            out_specs=[pl.BlockSpec((step, WIDE + 2 * HALF), lambda k, place: (k, 0))] * len(shifts),
        ),
        out_shape=[jax.ShapeDtypeStruct((tokens, WIDE + 2 * HALF), BF)] * len(shifts),
        compiler_params=pltpu.CompilerParams(vmem_limit_bytes=56 * 2**20),
        cost_estimate=pl.CostEstimate(
            flops=tokens * width, bytes_accessed=4 * tokens * width, transcendentals=0
        ),
        name="pack",
    )(place, hidden, cotangent)


def flip(blocks, core, flipped):
    tokens = blocks[0].shape[0]
    half = pl.ds(pl.multiple_of(WIDE + core * HALF, HALF // 2), HALF)
    for b in range(0, NX, 2):
        pair = jnp.concatenate([blocks[b][:, half], blocks[b + 1][:, half]], axis=0)
        flipped[:, b * tokens : (b + 2) * tokens] = pair.T


def other_kernel(place, *refs):
    *blocks, out, flipped = refs
    flip(blocks, 1 - place[0], flipped)
    for g in range(NZ // ZG):
        cols = slice(g * ZG * XROWS, (g + 1) * ZG * XROWS)
        rows = jnp.concatenate([block[:, cols] for block in blocks], axis=0)
        out[:, cols] = jnp.dot(flipped[...], rows, preferred_element_type=F32).astype(BF)


def own_kernel(place, *refs):
    *blocks, sent, perm, out, flipped = refs
    flip(blocks, place[0], flipped)
    for g in range(NZ // ZG):
        cols = slice(g * ZG * XROWS, (g + 1) * ZG * XROWS)
        rows = jnp.concatenate([block[:, cols] for block in blocks], axis=0)
        term = jnp.dot(flipped[...], rows, preferred_element_type=F32)
        term += sent[:, cols].astype(F32)
        moved = lax.dot_general(
            perm[...], term.astype(BF), (((1,), (1,)), ((), ())), preferred_element_type=F32
        ).astype(BF)
        out[:, g * ZG * ROWS : (g + 1) * ZG * ROWS] = moved.reshape(NY, ZG * ROWS, HALF)


def term_call(kernel, name, place, inputs, out_shape, tokens, weigh=1):
    whole = pl.BlockSpec(memory_space=pltpu.VMEM)
    return pl.pallas_call(
        kernel,
        grid_spec=pltpu.PrefetchScalarGridSpec(
            num_scalar_prefetch=1,
            grid=(1,),
            in_specs=[whole] * len(inputs),
            out_specs=pl.BlockSpec(out_shape, lambda k, place: (0,) * len(out_shape)),
            scratch_shapes=[pltpu.VMEM((HALF, NX * tokens), BF)],
        ),
        out_shape=jax.ShapeDtypeStruct(out_shape, BF),
        compiler_params=pltpu.CompilerParams(vmem_limit_bytes=24 * 2**20),
        cost_estimate=pl.CostEstimate(
            flops=weigh * 2 * WIDE * HALF * NX * tokens,
            bytes_accessed=2 * NX * tokens * (WIDE + 2 * HALF),
            transcendentals=0,
        ),
        name=name,
    )(place, *inputs)


def other_half(place, blocks):
    return term_call(other_kernel, "other_half", place, blocks, (HALF, WIDE), blocks[0].shape[0], 100)


def own_half(place, blocks, sent):
    inputs = [*blocks, sent, jnp.asarray(BY_DEVICE, BF)]
    return term_call(own_kernel, "own_half", place, inputs, (NY, NZ * ROWS, HALF), blocks[0].shape[0])


def regroup_kernel(parts, perm, out):
    rows = parts[...].reshape(ZROWS, HALF)
    out[...] = jnp.dot(perm[...], rows, preferred_element_type=F32).astype(BF).reshape(out.shape)


def regroup(parts):
    return pl.pallas_call(
        regroup_kernel,
        grid=(NZ // ZG,),
        in_specs=[
            pl.BlockSpec((NY, ZG * ROWS, HALF), lambda g: (0, g, 0)),
            pl.BlockSpec((ZROWS, ZROWS), lambda g: (0, 0)),
        ],
        out_specs=pl.BlockSpec((ZG, XROWS, HALF), lambda g: (g, 0, 0)),
        out_shape=jax.ShapeDtypeStruct((NZ, XROWS, HALF), BF),
        compiler_params=pltpu.CompilerParams(vmem_limit_bytes=12 * 2**20),
        cost_estimate=pl.CostEstimate(
            flops=2 * NZ // ZG * ZROWS * ZROWS * HALF,
            bytes_accessed=4 * NZ * XROWS * HALF,
            transcendentals=0,
        ),
        name="regroup",
    )(parts, jnp.asarray(IN_ORDER, BF))


def sum_y_kernel(parts, out):
    total = parts[0].astype(F32)
    for k in range(1, NY):
        total += parts[k].astype(F32)
    for z in range(NZ):
        out[z] = total[z * ROWS : (z + 1) * ROWS].astype(BF)


def sum_over_y(parts):
    return pl.pallas_call(
        sum_y_kernel,
        out_shape=jax.ShapeDtypeStruct((NZ, ROWS, HALF), BF),
        compiler_params=pltpu.CompilerParams(vmem_limit_bytes=12 * 2**20),
        name="sum_over_y",
    )(parts)


def project_kernel(place, *refs):
    *blocks, hidden, cot_mine, cot_other, keys, grad, acc, cot, held = refs
    step = pl.program_id(0)

    @pl.when(step == 0)
    def _():
        cot[:, :HALF] = cot_mine[...]
        cot[:, HALF:] = cot_other[...]
        acc[...] = jnp.zeros_like(acc)

    total = acc[...]
    for k in range(ZSTEP):
        for b, r in enumerate(HELD):
            x = lax.rem(place[1] + NX - r, NX)
            rows = pl.ds(pl.multiple_of(x * XROWS, XROWS), XROWS)
            held[k, rows, :HALF] = blocks[b][k]
            held[k, rows, HALF:] = blocks[NX + b][k]
        weight = held[k]
        cols = slice(k * ZROWS, (k + 1) * ZROWS)
        total += jnp.dot(hidden[:, cols], weight, preferred_element_type=F32)
        grad[:, cols] = lax.dot_general(
            cot[...], weight, (((1,), (1,)), ((), ())), preferred_element_type=F32
        ).astype(BF)
    acc[...] = total

    @pl.when((step == NZ // ZSTEP - 1) & (place[0] == 0))
    def _():
        keys[...] = acc[...].astype(BF)

    @pl.when((step == NZ // ZSTEP - 1) & (place[0] == 1))
    def _():
        keys[:, :HALF] = acc[:, HALF:].astype(BF)
        keys[:, HALF:] = acc[:, :HALF].astype(BF)


def project(place, mine, other, hidden, cotangent):
    tokens, width = hidden.shape
    block = pl.BlockSpec((ZSTEP, XROWS, HALF), lambda z, place: (z, 0, 0))
    wide = pl.BlockSpec((tokens, ZSTEP * ZROWS), lambda z, place: (0, z))
    return pl.pallas_call(
        project_kernel,
        grid_spec=pltpu.PrefetchScalarGridSpec(
            num_scalar_prefetch=1,
            grid=(NZ // ZSTEP,),
            in_specs=[block] * (2 * NX)
            + [
                wide,
                pl.BlockSpec((tokens, HALF), lambda z, place: (0, place[0])),
                pl.BlockSpec((tokens, HALF), lambda z, place: (0, 1 - place[0])),
            ],
            out_specs=[
                pl.BlockSpec((tokens, 2 * HALF), lambda z, place: (0, 0)),
                wide,
            ],
            scratch_shapes=[
                pltpu.VMEM((tokens, 2 * HALF), F32),
                pltpu.VMEM((tokens, 2 * HALF), BF),
                pltpu.VMEM((ZSTEP, ZROWS, 2 * HALF), BF),
            ],
        ),
        out_shape=[
            jax.ShapeDtypeStruct((tokens, 2 * HALF), BF),
            jax.ShapeDtypeStruct((tokens, width), BF),
        ],
        compiler_params=pltpu.CompilerParams(vmem_limit_bytes=16 * 2**20),
        cost_estimate=pl.CostEstimate(
            flops=8 * width * HALF * tokens,
            bytes_accessed=4 * tokens * width + 4 * width * HALF,
            transcendentals=0,
        ),
        name="project",
    )(place, *mine, *other, hidden, cotangent, cotangent)


def shard_kernel(values, scales, out):
    rows = lax.broadcasted_iota(jnp.int32, (ROWS, ROWS), 0)
    cols = lax.broadcasted_iota(jnp.int32, (ROWS, ROWS), 1)
    line = jnp.broadcast_to(scales[...].astype(F32), (ROWS, ROWS))
    column = jnp.sum(jnp.where(rows == cols, line, 0.0), axis=1, keepdims=True)
    shard = (values[...].astype(F32) * column).astype(BF)
    for z in range(NZ):
        out[z] = shard


def scaled_copies(values, scales):
    return pl.pallas_call(
        shard_kernel,
        out_shape=jax.ShapeDtypeStruct((NZ, ROWS, HALF), BF),
        compiler_params=pltpu.CompilerParams(vmem_limit_bytes=56 * 2**20),
        name="scaled_copies",
    )(values, scales.reshape(1, ROWS))


def to_all(piece, axis, count):
    copies = jnp.broadcast_to(piece[None], (count, *piece.shape))
    return lax.all_to_all(copies, axis, split_axis=0, concat_axis=0, tiled=True)


def shift(piece, r):
    return lax.ppermute(piece, "x", [(k, (k + r) % NX) for k in range(NX)])


def swap(piece):
    return lax.ppermute(piece, "c", [(0, 1), (1, 0)])


def on_device(hidden, cotangent, quant_weight, scales):
    place = jnp.stack([lax.axis_index("c"), lax.axis_index("x")]).astype(jnp.int32)
    factor = 1.0 / math.sqrt(hidden.shape[0] * NZ * NX * NY * NC)

    kept, far = pack(place, hidden, cotangent, (0, 2))

    values, _ = lax.optimization_barrier((quant_weight, far))
    copies = scaled_copies(values, scales)
    w_z = lax.all_to_all(copies, "z", split_axis=0, concat_axis=0, tiled=True)
    late, _ = lax.optimization_barrier((hidden, copies))
    near = pack(place, late, cotangent, (1, 3))
    w_z, near = lax.optimization_barrier((w_z, near))
    held = [kept, shift(far, 2), shift(near[0], 1), shift(near[1], 3)]
    ahead = other_half(place, held)
    term = own_half(place, held, swap(ahead))

    w_y = to_all(w_z.reshape(NZ * ROWS, HALF), Y, NY)

    own = regroup(lax.optimization_barrier((w_y, term))[0])
    mine = [own] + [shift(own, r) for r in HELD[1:]]
    other = [swap(piece) for piece in mine]

    t_y = lax.all_to_all(term, Y, split_axis=0, concat_axis=0, tiled=True)
    sum_y = sum_over_y(t_y)
    t_z = lax.all_to_all(sum_y, "z", split_axis=0, concat_axis=0, tiled=True)
    weight_grad = t_z.astype(F32).sum(0) * factor
    keys, grad_input = project(place, mine, other, hidden, cotangent)
    return keys, grad_input, weight_grad


def solution(mesh):
    fine = Mesh(mesh.devices.reshape(NZ, NX, NYH, NYL, NC), ("z", "x", "yh", "yl", "c"))
    node, local = ("z", "x", "yh"), ("yl", "c")
    return jax.shard_map(
        on_device,
        mesh=fine,
        in_specs=(P(node + local, None), P(node + local, None), P(node, local), P(node)),
        out_specs=(P(node + local, None), P(node + local, None), P(node, local)),
        check_vma=False,
    )
```

```python
import functools
import math

import jax
import jax.numpy as jnp
import numpy as np
from jax import lax
from jax.experimental import pallas as pl
from jax.experimental.pallas import tpu as pltpu
from jax.sharding import Mesh
from jax.sharding import PartitionSpec as P

NZ, NX, NYH, NYL, NC = 12, 4, 2, 4, 2
NY = NYH * NYL
Y = ("yh", "yl")
ROWS = 12
HALF = 256
ZROWS = NX * NY * ROWS
XROWS = NY * ROWS
WIDE = NZ * XROWS

BF = jnp.bfloat16
F32 = jnp.float32

ZG = 4
_z, _yh, _i, _yl = np.meshgrid(
    np.arange(ZG), np.arange(NYH), np.arange(ROWS), np.arange(NYL), indexing="ij"
)
BY_DEVICE = np.zeros((ZG * XROWS, ZG * XROWS), np.float32)
BY_DEVICE[(((_yh * NYL + _yl) * ZG + _z) * ROWS + _i).ravel(), np.arange(ZG * XROWS)] = 1
IN_ORDER = BY_DEVICE.T
HELD = (0, 2, 1, 3)
ZSTEP = 3


def pack_kernel(shifts, place, hidden, cot, *outs):
    for me in range(NX):

        @pl.when(place[1] == me)
        def _():
            for out, r in zip(outs, shifts):
                x = (me + r) % NX
                for g in range(NZ // ZG):
                    starts = [z * ZROWS + x * XROWS for z in range(g * ZG, (g + 1) * ZG)]
                    out[:, g * ZG * XROWS : (g + 1) * ZG * XROWS] = jnp.concatenate(
                        [hidden[:, start : start + XROWS] for start in starts], axis=1
                    )

    for out in outs:
        out[:, WIDE:] = cot[...]


def pack(place, hidden, cotangent, shifts):
    tokens, width = hidden.shape
    step = tokens // 2
    return pl.pallas_call(
        functools.partial(pack_kernel, shifts),
        grid_spec=pltpu.PrefetchScalarGridSpec(
            num_scalar_prefetch=1,
            grid=(2,),
            in_specs=[
                pl.BlockSpec((step, width), lambda k, place: (k, 0)),
                pl.BlockSpec((step, 2 * HALF), lambda k, place: (k, 0)),
            ],
            out_specs=[pl.BlockSpec((step, WIDE + 2 * HALF), lambda k, place: (k, 0))] * len(shifts),
        ),
        out_shape=[jax.ShapeDtypeStruct((tokens, WIDE + 2 * HALF), BF)] * len(shifts),
        compiler_params=pltpu.CompilerParams(vmem_limit_bytes=56 * 2**20),
        cost_estimate=pl.CostEstimate(
            flops=tokens * width, bytes_accessed=4 * tokens * width, transcendentals=0
        ),
        name="pack",
    )(place, hidden, cotangent)


def flip(blocks, core, flipped):
    tokens = blocks[0].shape[0]
    half = pl.ds(pl.multiple_of(WIDE + core * HALF, HALF // 2), HALF)
    for b in range(0, NX, 2):
        pair = jnp.concatenate([blocks[b][:, half], blocks[b + 1][:, half]], axis=0)
        flipped[:, b * tokens : (b + 2) * tokens] = pair.T


def other_kernel(place, *refs):
    *blocks, out, flipped = refs
    flip(blocks, 1 - place[0], flipped)
    for g in range(NZ // ZG):
        cols = slice(g * ZG * XROWS, (g + 1) * ZG * XROWS)
        rows = jnp.concatenate([block[:, cols] for block in blocks], axis=0)
        out[:, cols] = jnp.dot(flipped[...], rows, preferred_element_type=F32).astype(BF)


def own_kernel(place, *refs):
    *blocks, sent, perm, out, flipped = refs
    flip(blocks, place[0], flipped)
    for g in range(NZ // ZG):
        cols = slice(g * ZG * XROWS, (g + 1) * ZG * XROWS)
        rows = jnp.concatenate([block[:, cols] for block in blocks], axis=0)
        term = jnp.dot(flipped[...], rows, preferred_element_type=F32)
        term += sent[:, cols].astype(F32)
        moved = lax.dot_general(
            perm[...], term.astype(BF), (((1,), (1,)), ((), ())), preferred_element_type=F32
        ).astype(BF)
        out[:, g * ZG * ROWS : (g + 1) * ZG * ROWS] = moved.reshape(NY, ZG * ROWS, HALF)


def term_call(kernel, name, place, inputs, out_shape, tokens, weigh=1):
    whole = pl.BlockSpec(memory_space=pltpu.VMEM)
    return pl.pallas_call(
        kernel,
        grid_spec=pltpu.PrefetchScalarGridSpec(
            num_scalar_prefetch=1,
            grid=(1,),
            in_specs=[whole] * len(inputs),
            out_specs=pl.BlockSpec(out_shape, lambda k, place: (0,) * len(out_shape)),
            scratch_shapes=[pltpu.VMEM((HALF, NX * tokens), BF)],
        ),
        out_shape=jax.ShapeDtypeStruct(out_shape, BF),
        compiler_params=pltpu.CompilerParams(vmem_limit_bytes=24 * 2**20),
        cost_estimate=pl.CostEstimate(
            flops=weigh * 2 * WIDE * HALF * NX * tokens,
            bytes_accessed=2 * NX * tokens * (WIDE + 2 * HALF),
            transcendentals=0,
        ),
        name=name,
    )(place, *inputs)


def other_half(place, blocks):
    return term_call(other_kernel, "other_half", place, blocks, (HALF, WIDE), blocks[0].shape[0], 100)


def own_half(place, blocks, sent):
    inputs = [*blocks, sent, jnp.asarray(BY_DEVICE, BF)]
    return term_call(own_kernel, "own_half", place, inputs, (NY, NZ * ROWS, HALF), blocks[0].shape[0])


def regroup_kernel(parts, perm, out):
    rows = parts[...].reshape(ZROWS, HALF)
    out[...] = jnp.dot(perm[...], rows, preferred_element_type=F32).astype(BF).reshape(out.shape)


def regroup(parts):
    return pl.pallas_call(
        regroup_kernel,
        grid=(NZ // ZG,),
        in_specs=[
            pl.BlockSpec((NY, ZG * ROWS, HALF), lambda g: (0, g, 0)),
            pl.BlockSpec((ZROWS, ZROWS), lambda g: (0, 0)),
        ],
        out_specs=pl.BlockSpec((ZG, XROWS, HALF), lambda g: (g, 0, 0)),
        out_shape=jax.ShapeDtypeStruct((NZ, XROWS, HALF), BF),
        compiler_params=pltpu.CompilerParams(vmem_limit_bytes=12 * 2**20),
        cost_estimate=pl.CostEstimate(
            flops=2 * NZ // ZG * ZROWS * ZROWS * HALF,
            bytes_accessed=4 * NZ * XROWS * HALF,
            transcendentals=0,
        ),
        name="regroup",
    )(parts, jnp.asarray(IN_ORDER, BF))


def sum_y_kernel(parts, out):
    total = parts[0].astype(F32)
    for k in range(1, NY):
        total += parts[k].astype(F32)
    for z in range(NZ):
        out[z] = total[z * ROWS : (z + 1) * ROWS].astype(BF)


def sum_over_y(parts):
    return pl.pallas_call(
        sum_y_kernel,
        out_shape=jax.ShapeDtypeStruct((NZ, ROWS, HALF), BF),
        compiler_params=pltpu.CompilerParams(vmem_limit_bytes=12 * 2**20),
        name="sum_over_y",
    )(parts)


def project_kernel(place, *refs):
    *blocks, hidden, cot_mine, cot_other, keys, grad, acc, cot, held = refs
    step = pl.program_id(0)

    @pl.when(step == 0)
    def _():
        cot[:, :HALF] = cot_mine[...]
        cot[:, HALF:] = cot_other[...]
        acc[...] = jnp.zeros_like(acc)

    total = acc[...]
    for k in range(ZSTEP):
        for b, r in enumerate(HELD):
            x = lax.rem(place[1] + NX - r, NX)
            rows = pl.ds(pl.multiple_of(x * XROWS, XROWS), XROWS)
            held[k, rows, :HALF] = blocks[b][k]
            held[k, rows, HALF:] = blocks[NX + b][k]
        weight = held[k]
        cols = slice(k * ZROWS, (k + 1) * ZROWS)
        total += jnp.dot(hidden[:, cols], weight, preferred_element_type=F32)
        grad[:, cols] = lax.dot_general(
            cot[...], weight, (((1,), (1,)), ((), ())), preferred_element_type=F32
        ).astype(BF)
    acc[...] = total

    @pl.when((step == NZ // ZSTEP - 1) & (place[0] == 0))
    def _():
        keys[...] = acc[...].astype(BF)

    @pl.when((step == NZ // ZSTEP - 1) & (place[0] == 1))
    def _():
        keys[:, :HALF] = acc[:, HALF:].astype(BF)
        keys[:, HALF:] = acc[:, :HALF].astype(BF)


def project(place, mine, other, hidden, cotangent):
    tokens, width = hidden.shape
    block = pl.BlockSpec((ZSTEP, XROWS, HALF), lambda z, place: (z, 0, 0))
    wide = pl.BlockSpec((tokens, ZSTEP * ZROWS), lambda z, place: (0, z))
    return pl.pallas_call(
        project_kernel,
        grid_spec=pltpu.PrefetchScalarGridSpec(
            num_scalar_prefetch=1,
            grid=(NZ // ZSTEP,),
            in_specs=[block] * (2 * NX)
            + [
                wide,
                pl.BlockSpec((tokens, HALF), lambda z, place: (0, place[0])),
                pl.BlockSpec((tokens, HALF), lambda z, place: (0, 1 - place[0])),
            ],
            out_specs=[
                pl.BlockSpec((tokens, 2 * HALF), lambda z, place: (0, 0)),
                wide,
            ],
            scratch_shapes=[
                pltpu.VMEM((tokens, 2 * HALF), F32),
                pltpu.VMEM((tokens, 2 * HALF), BF),
                pltpu.VMEM((ZSTEP, ZROWS, 2 * HALF), BF),
            ],
        ),
        out_shape=[
            jax.ShapeDtypeStruct((tokens, 2 * HALF), BF),
            jax.ShapeDtypeStruct((tokens, width), BF),
        ],
        compiler_params=pltpu.CompilerParams(vmem_limit_bytes=16 * 2**20),
        cost_estimate=pl.CostEstimate(
            flops=8 * width * HALF * tokens,
            bytes_accessed=4 * tokens * width + 4 * width * HALF,
            transcendentals=0,
        ),
        name="project",
    )(place, *mine, *other, hidden, cotangent, cotangent)


def shard_kernel(values, scales, out):
    rows = lax.broadcasted_iota(jnp.int32, (ROWS, ROWS), 0)
    cols = lax.broadcasted_iota(jnp.int32, (ROWS, ROWS), 1)
    line = jnp.broadcast_to(scales[...].astype(F32), (ROWS, ROWS))
    column = jnp.sum(jnp.where(rows == cols, line, 0.0), axis=1, keepdims=True)
    shard = (values[...].astype(F32) * column).astype(BF)
    for z in range(NZ):
        out[z] = shard


def scaled_copies(values, scales):
    return pl.pallas_call(
        shard_kernel,
        out_shape=jax.ShapeDtypeStruct((NZ, ROWS, HALF), BF),
        compiler_params=pltpu.CompilerParams(vmem_limit_bytes=56 * 2**20),
        name="scaled_copies",
    )(values, scales.reshape(1, ROWS))


def to_all(piece, axis, count):
    copies = jnp.broadcast_to(piece[None], (count, *piece.shape))
    return lax.all_to_all(copies, axis, split_axis=0, concat_axis=0, tiled=True)


def shift(piece, r):
    return lax.ppermute(piece, "x", [(k, (k + r) % NX) for k in range(NX)])


def swap(piece):
    return lax.ppermute(piece, "c", [(0, 1), (1, 0)])


def on_device(hidden, cotangent, quant_weight, scales):
    place = jnp.stack([lax.axis_index("c"), lax.axis_index("x")]).astype(jnp.int32)
    factor = 1.0 / math.sqrt(hidden.shape[0] * NZ * NX * NY * NC)

    kept, far = pack(place, hidden, cotangent, (0, 2))

    values, _ = lax.optimization_barrier((quant_weight, far))
    copies = scaled_copies(values, scales)
    w_z = lax.all_to_all(copies, "z", split_axis=0, concat_axis=0, tiled=True)
    late, _ = lax.optimization_barrier((hidden, copies))
    near = pack(place, late, cotangent, (1, 3))
    w_z, near = lax.optimization_barrier((w_z, near))
    held = [kept, shift(far, 2), shift(near[0], 1), shift(near[1], 3)]
    ahead = other_half(place, held)
    term = own_half(place, held, swap(ahead))

    w_y = to_all(w_z.reshape(NZ * ROWS, HALF), Y, NY)

    own = regroup(lax.optimization_barrier((w_y, ahead))[0])
    mine = [own] + [shift(own, r) for r in HELD[1:]]
    other = [swap(piece) for piece in mine]

    t_y = lax.all_to_all(term, Y, split_axis=0, concat_axis=0, tiled=True)
    sum_y = sum_over_y(t_y)
    t_z = lax.all_to_all(sum_y, "z", split_axis=0, concat_axis=0, tiled=True)
    weight_grad = t_z.astype(F32).sum(0) * factor
    keys, grad_input = project(place, mine, other, hidden, cotangent)
    return keys, grad_input, weight_grad


def solution(mesh):
    fine = Mesh(mesh.devices.reshape(NZ, NX, NYH, NYL, NC), ("z", "x", "yh", "yl", "c"))
    node, local = ("z", "x", "yh"), ("yl", "c")
    return jax.shard_map(
        on_device,
        mesh=fine,
        in_specs=(P(node + local, None), P(node + local, None), P(node, local), P(node)),
        out_specs=(P(node + local, None), P(node + local, None), P(node, local)),
        check_vma=False,
    )
```

```python
import functools
import math

import jax
import jax.numpy as jnp
import numpy as np
from jax import lax
from jax.experimental import pallas as pl
from jax.experimental.pallas import tpu as pltpu
from jax.sharding import Mesh
from jax.sharding import PartitionSpec as P

NZ, NX, NYH, NYL, NC = 12, 4, 2, 4, 2
NY = NYH * NYL
Y = ("yh", "yl")
ROWS = 12
HALF = 256
ZROWS = NX * NY * ROWS
XROWS = NY * ROWS
WIDE = NZ * XROWS

BF = jnp.bfloat16
F32 = jnp.float32

ZG = 4
_z, _yh, _i, _yl = np.meshgrid(
    np.arange(ZG), np.arange(NYH), np.arange(ROWS), np.arange(NYL), indexing="ij"
)
BY_DEVICE = np.zeros((ZG * XROWS, ZG * XROWS), np.float32)
BY_DEVICE[(((_yh * NYL + _yl) * ZG + _z) * ROWS + _i).ravel(), np.arange(ZG * XROWS)] = 1
IN_ORDER = BY_DEVICE.T
HELD = (0, 3, 1, 2)
ZSTEP = 3


def pack_kernel(shifts, place, hidden, cot, *outs):
    for me in range(NX):

        @pl.when(place[1] == me)
        def _():
            for out, r in zip(outs, shifts):
                x = (me + r) % NX
                for g in range(NZ // ZG):
                    starts = [z * ZROWS + x * XROWS for z in range(g * ZG, (g + 1) * ZG)]
                    out[:, g * ZG * XROWS : (g + 1) * ZG * XROWS] = jnp.concatenate(
                        [hidden[:, start : start + XROWS] for start in starts], axis=1
                    )

    for out in outs:
        out[:, WIDE:] = cot[...]


def pack(place, hidden, cotangent, shifts):
    tokens, width = hidden.shape
    step = tokens // 2
    return pl.pallas_call(
        functools.partial(pack_kernel, shifts),
        grid_spec=pltpu.PrefetchScalarGridSpec(
            num_scalar_prefetch=1,
            grid=(2,),
            in_specs=[
                pl.BlockSpec((step, width), lambda k, place: (k, 0)),
                pl.BlockSpec((step, 2 * HALF), lambda k, place: (k, 0)),
            ],
            out_specs=[pl.BlockSpec((step, WIDE + 2 * HALF), lambda k, place: (k, 0))] * len(shifts),
        ),
        out_shape=[jax.ShapeDtypeStruct((tokens, WIDE + 2 * HALF), BF)] * len(shifts),
        compiler_params=pltpu.CompilerParams(vmem_limit_bytes=56 * 2**20),
        cost_estimate=pl.CostEstimate(
            flops=tokens * width, bytes_accessed=4 * tokens * width, transcendentals=0
        ),
        name="pack",
    )(place, hidden, cotangent)


def flip(blocks, core, flipped):
    tokens = blocks[0].shape[0]
    half = pl.ds(pl.multiple_of(WIDE + core * HALF, HALF // 2), HALF)
    for b in range(0, NX, 2):
        pair = jnp.concatenate([blocks[b][:, half], blocks[b + 1][:, half]], axis=0)
        flipped[:, b * tokens : (b + 2) * tokens] = pair.T


def other_kernel(place, *refs):
    *blocks, out, flipped = refs
    flip(blocks, 1 - place[0], flipped)
    for g in range(NZ // ZG):
        cols = slice(g * ZG * XROWS, (g + 1) * ZG * XROWS)
        rows = jnp.concatenate([block[:, cols] for block in blocks], axis=0)
        out[:, cols] = jnp.dot(flipped[...], rows, preferred_element_type=F32).astype(BF)


def own_kernel(place, *refs):
    *blocks, sent, perm, out, flipped = refs
    flip(blocks, place[0], flipped)
    for g in range(NZ // ZG):
        cols = slice(g * ZG * XROWS, (g + 1) * ZG * XROWS)
        rows = jnp.concatenate([block[:, cols] for block in blocks], axis=0)
        term = jnp.dot(flipped[...], rows, preferred_element_type=F32)
        term += sent[:, cols].astype(F32)
        moved = lax.dot_general(
            perm[...], term.astype(BF), (((1,), (1,)), ((), ())), preferred_element_type=F32
        ).astype(BF)
        out[:, g * ZG * ROWS : (g + 1) * ZG * ROWS] = moved.reshape(NY, ZG * ROWS, HALF)


def term_call(kernel, name, place, inputs, out_shape, tokens, weigh=1):
    whole = pl.BlockSpec(memory_space=pltpu.VMEM)
    return pl.pallas_call(
        kernel,
        grid_spec=pltpu.PrefetchScalarGridSpec(
            num_scalar_prefetch=1,
            grid=(1,),
            in_specs=[whole] * len(inputs),
            out_specs=pl.BlockSpec(out_shape, lambda k, place: (0,) * len(out_shape)),
            scratch_shapes=[pltpu.VMEM((HALF, NX * tokens), BF)],
        ),
        out_shape=jax.ShapeDtypeStruct(out_shape, BF),
        compiler_params=pltpu.CompilerParams(vmem_limit_bytes=24 * 2**20),
        cost_estimate=pl.CostEstimate(
            flops=weigh * 2 * WIDE * HALF * NX * tokens,
            bytes_accessed=2 * NX * tokens * (WIDE + 2 * HALF),
            transcendentals=0,
        ),
        name=name,
    )(place, *inputs)


def other_half(place, blocks):
    return term_call(other_kernel, "other_half", place, blocks, (HALF, WIDE), blocks[0].shape[0], 100)


def own_half(place, blocks, sent):
    inputs = [*blocks, sent, jnp.asarray(BY_DEVICE, BF)]
    return term_call(own_kernel, "own_half", place, inputs, (NY, NZ * ROWS, HALF), blocks[0].shape[0])


def regroup_kernel(parts, perm, out):
    rows = parts[...].reshape(ZROWS, HALF)
    out[...] = jnp.dot(perm[...], rows, preferred_element_type=F32).astype(BF).reshape(out.shape)


def regroup(parts):
    return pl.pallas_call(
        regroup_kernel,
        grid=(NZ // ZG,),
        in_specs=[
            pl.BlockSpec((NY, ZG * ROWS, HALF), lambda g: (0, g, 0)),
            pl.BlockSpec((ZROWS, ZROWS), lambda g: (0, 0)),
        ],
        out_specs=pl.BlockSpec((ZG, XROWS, HALF), lambda g: (g, 0, 0)),
        out_shape=jax.ShapeDtypeStruct((NZ, XROWS, HALF), BF),
        compiler_params=pltpu.CompilerParams(vmem_limit_bytes=12 * 2**20),
        cost_estimate=pl.CostEstimate(
            flops=2 * NZ // ZG * ZROWS * ZROWS * HALF,
            bytes_accessed=4 * NZ * XROWS * HALF,
            transcendentals=0,
        ),
        name="regroup",
    )(parts, jnp.asarray(IN_ORDER, BF))


def sum_y_kernel(parts, out):
    total = parts[0].astype(F32)
    for k in range(1, NY):
        total += parts[k].astype(F32)
    for z in range(NZ):
        out[z] = total[z * ROWS : (z + 1) * ROWS].astype(BF)


def sum_over_y(parts):
    return pl.pallas_call(
        sum_y_kernel,
        out_shape=jax.ShapeDtypeStruct((NZ, ROWS, HALF), BF),
        compiler_params=pltpu.CompilerParams(vmem_limit_bytes=12 * 2**20),
        name="sum_over_y",
    )(parts)


def project_kernel(place, *refs):
    *blocks, hidden, cot_mine, cot_other, keys, grad, acc, cot, held = refs
    step = pl.program_id(0)

    @pl.when(step == 0)
    def _():
        cot[:, :HALF] = cot_mine[...]
        cot[:, HALF:] = cot_other[...]
        acc[...] = jnp.zeros_like(acc)

    total = acc[...]
    for k in range(ZSTEP):
        for b, r in enumerate(HELD):
            x = lax.rem(place[1] + NX - r, NX)
            rows = pl.ds(pl.multiple_of(x * XROWS, XROWS), XROWS)
            held[k, rows, :HALF] = blocks[b][k]
            held[k, rows, HALF:] = blocks[NX + b][k]
        weight = held[k]
        cols = slice(k * ZROWS, (k + 1) * ZROWS)
        total += jnp.dot(hidden[:, cols], weight, preferred_element_type=F32)
        grad[:, cols] = lax.dot_general(
            cot[...], weight, (((1,), (1,)), ((), ())), preferred_element_type=F32
        ).astype(BF)
    acc[...] = total

    @pl.when((step == NZ // ZSTEP - 1) & (place[0] == 0))
    def _():
        keys[...] = acc[...].astype(BF)

    @pl.when((step == NZ // ZSTEP - 1) & (place[0] == 1))
    def _():
        keys[:, :HALF] = acc[:, HALF:].astype(BF)
        keys[:, HALF:] = acc[:, :HALF].astype(BF)


def project(place, mine, other, hidden, cotangent):
    tokens, width = hidden.shape
    block = pl.BlockSpec((ZSTEP, XROWS, HALF), lambda z, place: (z, 0, 0))
    wide = pl.BlockSpec((tokens, ZSTEP * ZROWS), lambda z, place: (0, z))
    return pl.pallas_call(
        project_kernel,
        grid_spec=pltpu.PrefetchScalarGridSpec(
            num_scalar_prefetch=1,
            grid=(NZ // ZSTEP,),
            in_specs=[block] * (2 * NX)
            + [
                wide,
                pl.BlockSpec((tokens, HALF), lambda z, place: (0, place[0])),
                pl.BlockSpec((tokens, HALF), lambda z, place: (0, 1 - place[0])),
            ],
            out_specs=[
                pl.BlockSpec((tokens, 2 * HALF), lambda z, place: (0, 0)),
                wide,
            ],
            scratch_shapes=[
                pltpu.VMEM((tokens, 2 * HALF), F32),
                pltpu.VMEM((tokens, 2 * HALF), BF),
                pltpu.VMEM((ZSTEP, ZROWS, 2 * HALF), BF),
            ],
        ),
        out_shape=[
            jax.ShapeDtypeStruct((tokens, 2 * HALF), BF),
            jax.ShapeDtypeStruct((tokens, width), BF),
        ],
        compiler_params=pltpu.CompilerParams(vmem_limit_bytes=16 * 2**20),
        cost_estimate=pl.CostEstimate(
            flops=8 * width * HALF * tokens,
            bytes_accessed=4 * tokens * width + 4 * width * HALF,
            transcendentals=0,
        ),
        name="project",
    )(place, *mine, *other, hidden, cotangent, cotangent)


def shard_kernel(values, scales, out):
    rows = lax.broadcasted_iota(jnp.int32, (ROWS, ROWS), 0)
    cols = lax.broadcasted_iota(jnp.int32, (ROWS, ROWS), 1)
    line = jnp.broadcast_to(scales[...].astype(F32), (ROWS, ROWS))
    column = jnp.sum(jnp.where(rows == cols, line, 0.0), axis=1, keepdims=True)
    shard = (values[...].astype(F32) * column).astype(BF)
    for z in range(NZ):
        out[z] = shard


def scaled_copies(values, scales):
    return pl.pallas_call(
        shard_kernel,
        out_shape=jax.ShapeDtypeStruct((NZ, ROWS, HALF), BF),
        compiler_params=pltpu.CompilerParams(vmem_limit_bytes=56 * 2**20),
        name="scaled_copies",
    )(values, scales.reshape(1, ROWS))


def to_all(piece, axis, count):
    copies = jnp.broadcast_to(piece[None], (count, *piece.shape))
    return lax.all_to_all(copies, axis, split_axis=0, concat_axis=0, tiled=True)


def shift(piece, r):
    return lax.ppermute(piece, "x", [(k, (k + r) % NX) for k in range(NX)])


def swap(piece):
    return lax.ppermute(piece, "c", [(0, 1), (1, 0)])


def on_device(hidden, cotangent, quant_weight, scales):
    place = jnp.stack([lax.axis_index("c"), lax.axis_index("x")]).astype(jnp.int32)
    factor = 1.0 / math.sqrt(hidden.shape[0] * NZ * NX * NY * NC)

    packed = pack(place, hidden, cotangent, range(NX))
    held = [packed[0]] + [shift(packed[r], r) for r in (2, 1, 3)]
    ahead = other_half(place, held)
    term = own_half(place, held, swap(ahead))

    values, _ = lax.optimization_barrier((quant_weight, packed[0]))
    copies = scaled_copies(values, scales)
    w_z = lax.all_to_all(copies, "z", split_axis=0, concat_axis=0, tiled=True)
    w_y = to_all(w_z.reshape(NZ * ROWS, HALF), Y, NY)

    own = regroup(lax.optimization_barrier((w_y, term))[0])
    mine = [own] + [shift(own, r) for r in HELD[1:]]
    other = [swap(piece) for piece in mine]

    t_y = lax.all_to_all(term, Y, split_axis=0, concat_axis=0, tiled=True)
    sum_y = sum_over_y(t_y)
    t_z = lax.all_to_all(sum_y, "z", split_axis=0, concat_axis=0, tiled=True)
    weight_grad = t_z.astype(F32).sum(0) * factor
    keys, grad_input = project(place, mine, other, hidden, cotangent)
    return keys, grad_input, weight_grad


def solution(mesh):
    fine = Mesh(mesh.devices.reshape(NZ, NX, NYH, NYL, NC), ("z", "x", "yh", "yl", "c"))
    node, local = ("z", "x", "yh"), ("yl", "c")
    return jax.shard_map(
        on_device,
        mesh=fine,
        in_specs=(P(node + local, None), P(node + local, None), P(node, local), P(node)),
        out_specs=(P(node + local, None), P(node + local, None), P(node, local)),
        check_vma=False,
    )
```
